256 devices in a mesh: hst: 32 (over z, x), tp: 8 (over y, core).
Axes of the slice: x: 4, y: 4, z: 8, core: 2. Of those that a mesh axis runs over, the one named last changes fastest.
Arguments:
- queries: bfloat16 [2048, 4096], P('hst', 'tp')
- key_page_cache: bfloat16 [16384, 16, 1024], P('hst', None, 'tp')
- value_page_cache: bfloat16 [16384, 16, 1024], P('hst', None, 'tp'), may hold values from -5 to 5
- request_pages: int32 [2048, 8], P('hst'), may hold values from 0 to 511, as said below
- context_length: int32 [2048], P('hst'), may hold values from 2 to 128, as said below
- output_weight: bfloat16 [4096, 4096], P('tp'), may hold values from -0.09375 to 0.09375
- adapter_down_weight: bfloat16 [1024, 64, 4096], P('hst', None, 'tp'), may hold values from -0.09375 to 0.09375
- adapter_up_weight: bfloat16 [1024, 64, 4096], P('hst', None, 'tp'), may hold values from -0.75 to 0.75
- residual: bfloat16 [2048, 4096], P('hst', 'tp'), may hold values from -6 to 6
- host_slot_adapter: int32 [1024], P('hst'), may hold values from 0 to 1023, as said below
- request_slot: int32 [2048, 1], P('hst'), may hold values from 0 to 31; in each aligned block of 64 rows (0 to 63, 64 to 127, ...) at most 4 rows name the same one
Outputs:
- hidden_out: bfloat16 [2048, 4096], P('hst', 'tp')
The draws below stay inside these ranges and needn't reach their ends.
Inputs may be any that keep to these rules, and one draw needn't show every extreme that they name: `request_pages`: entries of one host are its pages 512 in some order: every page of the host belongs to exactly one request. `context_length`: some request of every host has exactly 128 cached tokens. `host_slot_adapter`: A host's 32 entries name different adapters; adapter a is owned by host a // 32. No owner serves more than 2 slots of one host, and some owner serves exactly 2 slots of every host. `request_slot`: at most 4 of the rows of one host name one slot.
All inputs are finite; a program needn't handle non-finite values.
Results may differ from the reference program's by a relative error of at most 0.0085.
Values may be sent and summed in bfloat16 or wider, within the bound.
A program may use at most 128 MiB of HBM per device.

```python
import math
import jax
import jax.numpy as jnp
import numpy as np
from jax import lax

MODEL_WIDTH = 4096
H = 32
KVH = 8
HD = 128
ADAPTER_RANK = 64
PAGE = 16
SLOTS = 32
ROWS = 64
CTX = 128
ADP_HOST = 32
ADAPTER_TOTAL = 1024
ROWS_ALL = 2048
MAXP = 8
PAGES = 512
MOST = 2
CAP = 4
N_HST = 32


def page_order(key):
    subkey = jax.random.fold_in(key, 7)
    host_count = ADAPTER_TOTAL // ADP_HOST
    host_keys = jax.random.split(subkey, host_count)
    orders = jax.vmap(lambda one_key: jax.random.permutation(one_key, PAGES))(host_keys)
    return orders.reshape(host_count * ROWS, MAXP).astype(jnp.int32)


def draw_request_pages(key, part):
    return page_order(key)


def draw_key_page_cache(key, part):
    key = jax.random.fold_in(key, 23)
    host_count = ADAPTER_TOTAL // ADP_HOST
    keys_all = jnp.clip(jax.random.normal(key, (host_count * PAGES, PAGE, KVH * HD), jnp.float32), -4.0, 4.0)
    return keys_all.astype(jnp.bfloat16)


def draw_queries(key, part):
    key = jax.random.fold_in(key, 29)
    host_count = ADAPTER_TOTAL // ADP_HOST
    row_total = host_count * ROWS
    query_all = jnp.clip(jax.random.normal(key, (row_total, H * HD), jnp.float32), -4.0, 4.0)
    return query_all.astype(jnp.bfloat16)


def draw_context_length(key, part):
    key = jax.random.fold_in(key, 31)
    host_count = ADAPTER_TOTAL // ADP_HOST
    lengths = jax.random.randint(key, (host_count, ROWS), 2, CTX + 1)
    full_row = jax.random.randint(jax.random.fold_in(key, 1), (host_count,), 0, ROWS)
    lengths = jnp.where(jnp.arange(ROWS)[None, :] == full_row[:, None], CTX, lengths)
    return lengths.reshape(host_count * ROWS).astype(jnp.int32)


def draw_host_slot_adapter(key, part):
    key = jax.random.fold_in(key, 37)
    host_count = ADAPTER_TOTAL // ADP_HOST
    lowrank_stock_count = host_count * MOST
    lowrank_holder_device = jnp.arange(lowrank_stock_count) // MOST
    pool_copy = jnp.arange(lowrank_stock_count) % MOST
    preferred_machine = jax.random.randint(jax.random.fold_in(key, 1), (), 0, host_count)
    machine_leaning = jax.random.randint(jax.random.fold_in(key, 2), (host_count,), 0, 4)
    noise_perturbation = jax.random.randint(jax.random.fold_in(key, 3), (host_count, lowrank_stock_count), 0, 2 ** 15)
    liking_boost = machine_leaning[lowrank_holder_device] * 2 ** 14 + (lowrank_holder_device == preferred_machine).astype(jnp.int32) * 2 ** 20
    query_match_logits = (noise_perturbation + liking_boost[None, :]) * lowrank_stock_count + jnp.arange(lowrank_stock_count)[None, :]
    top_scores, picked_adapters = lax.top_k(query_match_logits, SLOTS)
    owners = lowrank_holder_device[picked_adapters]
    copies = pool_copy[picked_adapters]
    shifts = jax.random.randint(jax.random.fold_in(key, 4), (host_count, host_count), 0, ADP_HOST)
    offsets = jnp.take_along_axis(shifts, owners, axis=1)
    adapter_ids = owners * ADP_HOST + (copies + offsets) % ADP_HOST
    host_keys = jax.random.split(jax.random.fold_in(key, 5), host_count)
    shuffled = jax.vmap(lambda one_key, id_row: jax.random.permutation(one_key, id_row))(host_keys, adapter_ids)
    return shuffled.reshape(host_count * SLOTS).astype(jnp.int32)


def block_levels(own_key, dims, pieces, low, top_value):
    def one(dim, blocks):
        heights = jax.random.uniform(jax.random.fold_in(jax.random.fold_in(own_key, 6), dim), (blocks,), jnp.float32, low / len(pieces), top_value / len(pieces))
        return jnp.repeat(jnp.exp(heights), dims[dim] // blocks).reshape((-1,) + (1,) * (len(dims) - dim - 1))

    factor_of = one(*pieces[0])
    for cut in pieces[1:]:
        factor_of = factor_of * one(*cut)
    return factor_of


def assign_block(key, own, number, rows, number_of, top, limit, lean):
    sequence = jax.random.permutation(key, number_of)
    packed, usual = shares(number_of, rows * top, limit, lean, True), shares(number_of, rows * top, limit, lean, False)
    places = jnp.arange(number_of)

    def named(sizes, turn):
        used = int((sizes > 0).sum())
        fixed = max(1, used // 4)
        shifted = fixed + (places - fixed + turn * (used - fixed)) % max(1, number_of - fixed)
        return jnp.zeros((number_of,), jnp.int32).at[sequence[jnp.where(places < fixed, places, shifted)]].set(jnp.asarray(sizes, jnp.int32))

    sizes = jnp.where(number % 4 == 0, named(packed, number // 4), named(usual, number - number // 4 - 1))
    mixed = jax.random.permutation(jax.random.fold_in(own, 3), number_of)
    source_of, taker = mixed[0:number_of // 2 * 2:2], mixed[1:number_of // 2 * 2:2]
    slack = jnp.minimum(sizes[source_of] - 1, limit - sizes[taker]) // 2
    slack = jnp.where((source_of == sequence[0]) | (taker == sequence[0]) | (sizes[taker] == 0), 0, jnp.maximum(slack, 0))
    shifted = jax.random.randint(jax.random.fold_in(own, 4), (number_of // 2,), 0, 1 << 20) % (slack + 1)
    sizes = sizes.at[source_of].add(-shifted).at[taker].add(shifted)
    members = jnp.searchsorted(jnp.cumsum(sizes), jnp.arange(rows * top), side="right").astype(jnp.int32)
    listing = members.reshape(top, rows).T
    listing = listing[jax.random.permutation(jax.random.fold_in(own, 1), rows)]
    turn = jax.random.randint(jax.random.fold_in(own, 2), (rows, 1), 0, top)
    return jnp.take_along_axis(listing, (jnp.arange(top)[None, :] + turn) % top, axis=1)


def shares(amount, total, bound, skew, full):
    portions = [(1 << 20) // math.isqrt(grade ** skew) + 1 for grade in range(1, amount + 1)]
    largest = bound if full else min(bound, max(-(-total // amount), total * portions[0] // sum(portions)))
    least = 1 if total - largest >= amount - 1 else 0
    holding, surplus = [largest] + [least] * (amount - 1), total - largest - least * (amount - 1)
    while surplus > 0:
        movable = [i for i in range(1, amount) if holding[i] < largest] or [i for i in range(1, amount) if holding[i] < bound]
        mass, budget = sum([portions[i] for i in movable]), surplus
        for i in movable:
            more = min(bound - holding[i], max(1, budget * portions[i] // mass), surplus)
            holding[i] = holding[i] + more
            surplus = surplus - more
    return np.array(holding)


def noise(rng, extent, width, bound, pieces=(), held_as=jnp.bfloat16):
    result = jax.random.normal(rng, extent, jnp.float32) * width
    if len(pieces) > 0:
        result = block_levels(rng, extent, pieces, -0.22, 0.18) * result
    return jnp.clip(result, min=-bound, max=bound).astype(held_as)


def setup_inputs(seed: int = 0) -> dict:
    splits = jax.random.split(jax.random.key(seed), 12)
    queries = draw_queries(jax.random.fold_in(splits[11], 71), 0)
    key_page_cache = draw_key_page_cache(jax.random.fold_in(splits[11], 71), 0)
    value_page_cache = noise(splits[2], (N_HST * PAGES, PAGE, KVH * HD), 1.0, 5.0, ((0, 32), (2, 8)))
    request_pages = draw_request_pages(jax.random.fold_in(splits[11], 71), 0)
    context_length = draw_context_length(jax.random.fold_in(splits[11], 71), 0)
    output_weight = noise(splits[5], (MODEL_WIDTH, MODEL_WIDTH), MODEL_WIDTH ** -0.5, 0.09375, ((0, 8),))
    adapter_down_weight = noise(splits[6], (ADAPTER_TOTAL, ADAPTER_RANK, MODEL_WIDTH), MODEL_WIDTH ** -0.5, 0.09375, ((0, 32), (2, 8)))
    adapter_up_weight = noise(splits[7], (ADAPTER_TOTAL, ADAPTER_RANK, MODEL_WIDTH), ADAPTER_RANK ** -0.5, 0.75, ((0, 32), (2, 8)))
    residual = noise(splits[8], (ROWS_ALL, MODEL_WIDTH), 1.0, 6.0, ((0, 32), (1, 8)))
    host_slot_adapter = draw_host_slot_adapter(jax.random.fold_in(splits[11], 71), 0)
    request_slot_keys = jax.random.split(jax.random.fold_in(splits[10], 1), ROWS_ALL // ROWS)
    request_slot_turns = jax.random.permutation(jax.random.fold_in(splits[10], 3), ROWS_ALL // ROWS)
    request_slot = jax.vmap(lambda own, number: assign_block(jax.random.fold_in(splits[10], 2), own, number, ROWS, SLOTS, 1, CAP, 1))(request_slot_keys, request_slot_turns).reshape((ROWS_ALL, 1))
    return {"queries": queries, "key_page_cache": key_page_cache, "value_page_cache": value_page_cache, "request_pages": request_pages, "context_length": context_length, "output_weight": output_weight, "adapter_down_weight": adapter_down_weight, "adapter_up_weight": adapter_up_weight, "residual": residual, "host_slot_adapter": host_slot_adapter, "request_slot": request_slot}


ADAPTER_SCALE = 2.0

def reference(queries, key_page_cache, value_page_cache, request_pages, context_length, output_weight, adapter_down_weight, adapter_up_weight, residual, host_slot_adapter, request_slot):
    group_size = H // KVH

    def one_host(host_index):
        row_start = host_index * ROWS
        query_rows = lax.dynamic_slice_in_dim(queries, row_start, ROWS, 0).astype(jnp.float32).reshape(ROWS, KVH, group_size, HD)
        page_rows = lax.dynamic_slice_in_dim(request_pages, row_start, ROWS, 0) + host_index * PAGES
        key_rows = key_page_cache[page_rows].astype(jnp.float32).reshape(ROWS, CTX, KVH, HD)
        value_rows = value_page_cache[page_rows].astype(jnp.float32).reshape(ROWS, CTX, KVH, HD)
        lengths = lax.dynamic_slice_in_dim(context_length, row_start, ROWS, 0)
        query_match_logits = jnp.einsum('rkgd,rtkd->rkgt', query_rows, key_rows) / math.sqrt(HD)
        live_mask = jnp.arange(CTX)[None, :] < lengths[:, None]
        query_match_logits = jnp.where(live_mask[:, None, None, :], query_match_logits, -jnp.inf)
        attn_weights = jax.nn.softmax(query_match_logits, axis=-1).astype(jnp.bfloat16)
        attended = jnp.einsum('rkgt,rtkd->rkgd', attn_weights.astype(jnp.float32), value_rows)
        attended = attended.astype(jnp.bfloat16).reshape(ROWS, MODEL_WIDTH)
        slot_ids = lax.dynamic_slice_in_dim(host_slot_adapter, host_index * SLOTS, SLOTS, 0)
        chosen = lax.dynamic_slice_in_dim(request_slot, row_start, ROWS, 0)[:, 0]
        adapter_index = slot_ids[chosen]
        down_weight_rows = adapter_down_weight[adapter_index].astype(jnp.float32)
        reduced_activations = jnp.einsum('rd,rkd->rk', attended.astype(jnp.float32), down_weight_rows).astype(jnp.bfloat16)
        up_weight_rows = adapter_up_weight[adapter_index].astype(jnp.float32)
        adapter_rows = jnp.einsum('lw,lwn->ln', reduced_activations.astype(jnp.float32), up_weight_rows)
        base_output = jnp.dot(attended, output_weight, preferred_element_type=jnp.float32)
        residual_output_rows = lax.dynamic_slice_in_dim(residual, row_start, ROWS, 0).astype(jnp.float32)
        return (residual_output_rows + base_output + ADAPTER_SCALE * adapter_rows).astype(jnp.bfloat16)
    stacked = lax.map(one_host, jnp.arange(N_HST).astype(jnp.int32))
    return stacked.reshape(N_HST * ROWS, MODEL_WIDTH)
```

```python
import functools
import math

import jax
import jax.numpy as jnp
from jax import lax
from jax.experimental import pallas as pl
from jax.experimental.pallas import tpu as pltpu
from jax.sharding import PartitionSpec as P

HD = 128
ADAPTER_SCALE = 2.0
MESH = pl.DeviceIdType.MESH
BF = jnp.bfloat16
F32 = jnp.float32
NT = (((1,), (1,)), ((), ()))
NN = (((1,), (0,)), ((), ()))


def dot(a, b, dims=NN):
    return lax.dot_general(a, b, dims, preferred_element_type=F32)


def iota(shape, dim):
    return lax.broadcasted_iota(jnp.int32, shape, dim)


def kernel(
    n_hst,
    n_tp,
    q_hbm,
    k_hbm,
    v_hbm,
    pages_ref,
    length_ref,
    w_hbm,
    down_hbm,
    up_hbm,
    table_ref,
    slot_ref,
    out_ref,
    q_ref,
    k_ref,
    v_ref,
    w_ref,
    down_ref,
    up_ref,
    att_ref,
    table_out,
    tables,
    rows_out,
    rows_in,
    back_out,
    back_in,
    base_out,
    base_in,
    part_out,
    part_in,
    shrunk,
    local_sem,
    table_send,
    table_recv,
    rows_send,
    rows_recv,
    back_send,
    back_recv,
    base_send,
    base_recv,
    part_send,
    part_recv,
    shrunk_send,
    shrunk_recv,
):
    host = lax.axis_index("hst")
    lane = lax.axis_index("tp")

    def load(src, dst, i):
        return pltpu.make_async_copy(src, dst, local_sem.at[i])

    load_q = load(q_hbm, q_ref, 0)
    load_k = load(k_hbm, k_ref, 1)
    load_v = load(v_hbm, v_ref, 2)
    load_w = load(w_hbm, w_ref, 3)
    load_down = load(down_hbm, down_ref, 4)
    load_up = load(up_hbm, up_ref, 5)
    load_q.start()
    load_k.start()
    load_v.start()
    load_w.start()
    load_down.start()
    load_up.start()

    barrier = pltpu.get_barrier_semaphore()

    def greet_hosts(step, carry):
        other = lax.rem(host + step, n_hst)
        pl.semaphore_signal(barrier, inc=1, device_id=(other, lane), device_id_type=MESH)
        return carry

    def greet_lanes(step, carry):
        other = lax.rem(lane + step, n_tp)
        pl.semaphore_signal(barrier, inc=1, device_id=(host, other), device_id_type=MESH)
        return carry

    lax.fori_loop(1, n_hst, greet_hosts, 0)
    lax.fori_loop(1, n_tp, greet_lanes, 0)

    slots = table_ref.shape[1]
    row_total = slot_ref.shape[0]
    table_out[...] = jnp.full(table_out.shape, -1, jnp.int32)
    table_out[0:1, 0:slots] = table_ref[...]
    table_row = table_out[0:1, :]
    owner_row = jnp.right_shift(table_row, 5)
    owner_all = jnp.broadcast_to(owner_row, (128, 128))
    s_sub, s_lane = iota((128, 128), 0), iota((128, 128), 1)
    owner_col = jnp.sum(jnp.where(s_sub == s_lane, owner_all, 0), axis=1, keepdims=True)
    place_row = jnp.sum(
        jnp.where((owner_col == owner_all) & (s_sub < s_lane), 1, 0), axis=0, keepdims=True
    )
    start_row = owner_row * 8 + place_row * 4
    chosen_col = slot_ref[...]
    r_sub, r_lane = iota((row_total, 128), 0), iota((row_total, 128), 1)
    chosen_row = jnp.sum(jnp.where(r_sub == r_lane, chosen_col, 0), axis=0, keepdims=True)
    before_col = jnp.sum(
        jnp.where((chosen_col == chosen_row) & (r_lane < r_sub), 1, 0), axis=1, keepdims=True
    )
    target_col = before_col + jnp.sum(
        jnp.where(chosen_col == r_lane, start_row, 0), axis=1, keepdims=True
    )
    target_row = jnp.sum(jnp.where(r_sub == r_lane, target_col, 0), axis=0, keepdims=True)
    send_total = n_hst * 8
    scatter = jnp.where(
        iota((send_total, row_total), 0) == target_row[:, :row_total], 1.0, 0.0
    ).astype(BF)
    back_place = (target_col // 8) * 16 + lax.rem(target_col, 8)
    back_lane = iota((row_total, n_hst * 16), 1)
    gather_lo = jnp.where(back_lane == back_place, 1.0, 0.0).astype(BF)
    gather_hi = jnp.where(back_lane == back_place + 8, 1.0, 0.0).astype(BF)

    pl.semaphore_wait(barrier, n_hst - 1 + n_tp - 1)

    tables[pl.ds(host, 1), :] = table_row

    def table_copy(other, mine, step):
        return pltpu.make_async_remote_copy(
            src_ref=table_out.at[0:1, :],
            dst_ref=tables.at[pl.ds(mine, 1), :],
            send_sem=table_send.at[step],
            recv_sem=table_recv.at[step],
            device_id=(other, lane),
            device_id_type=MESH,
        )

    def send_table(step, carry):
        table_copy(lax.rem(host + step, n_hst), host, step).start()
        return carry

    lax.fori_loop(1, n_hst, send_table, 0)

    load_q.wait()
    load_k.wait()
    load_v.wait()
    heads = q_ref.shape[1] // HD
    tall = heads * 16
    member = lax.rem(iota((tall, HD), 0), 16)
    token = iota((tall, HD), 1)
    scale = 1.0 / math.sqrt(HD)

    def pages_of(ref, row):
        return [ref[pages_ref[row, p]] for p in range(pages_ref.shape[1])]

    def attend(group, carry):
        first = pl.multiple_of(group * 16, 16)
        q = q_ref[pl.ds(first, 16), :]
        q = jnp.concatenate([q[:, j * HD : (j + 1) * HD] for j in range(heads)], axis=0)
        logits = jnp.full((tall, HD), -jnp.inf, F32)
        for r in range(0, 16, 2):
            keys = jnp.concatenate(pages_of(k_ref, first + r) + pages_of(k_ref, first + r + 1), axis=0)
            s = dot(q, keys, NT)
            for i in range(2):
                live = (member == r + i) & (token < length_ref[first + r + i])
                logits = jnp.where(live, s[:, i * HD : (i + 1) * HD] * scale, logits)
        top = jnp.max(logits, axis=1, keepdims=True)
        e = jnp.exp(logits - top)
        p = e / jnp.sum(e, axis=1, keepdims=True)
        acc = jnp.zeros((tall, HD), F32)
        for r in range(0, 16, 2):
            values = jnp.concatenate(pages_of(v_ref, first + r) + pages_of(v_ref, first + r + 1), axis=0)
            spread = jnp.concatenate([jnp.where(member == r + i, p, 0.0) for i in range(2)], axis=1)
            acc = acc + dot(spread.astype(BF), values)
        acc = acc.astype(BF)
        for j in range(heads):
            att_ref[pl.ds(first, 16), j * HD : (j + 1) * HD] = acc[j * 16 : (j + 1) * 16]
        return carry

    lax.fori_loop(0, row_total // 16, attend, 0)

    att = att_ref[...]
    half = att.shape[1] // 2

    def pack(lo, hi):
        return jnp.concatenate(
            [lo.reshape(n_hst, 8, half), hi.reshape(n_hst, 8, half)], axis=1
        ).astype(BF)

    def unpack(x):
        x = x.astype(F32)
        return (
            x[:, :8].reshape(n_hst * 8, half).astype(BF),
            x[:, 8:].reshape(n_hst * 8, half).astype(BF),
        )

    rows_out[...] = pack(dot(scatter, att[:, :half]), dot(scatter, att[:, half:]))

    def block_copy(out, into, send_sem, recv_sem, other, mine, step):
        return pltpu.make_async_remote_copy(
            src_ref=out.at[other],
            dst_ref=into.at[mine],
            send_sem=send_sem.at[step],
            recv_sem=recv_sem.at[step],
            device_id=(other, lane),
            device_id_type=MESH,
        )

    def send_rows(step, carry):
        block_copy(
            rows_out, rows_in, rows_send, rows_recv, lax.rem(host + step, n_hst), host, step
        ).start()
        return carry

    lax.fori_loop(1, n_hst, send_rows, 0)
    rows_in[pl.ds(host, 1)] = rows_out[pl.ds(host, 1)]

    load_w.wait()
    width = out_ref.shape[1]

    def project(which):
        return dot(att, w_ref[:, pl.ds(pl.multiple_of(which * width, width), width)])

    def base_copy(other, step):
        return pltpu.make_async_remote_copy(
            src_ref=base_out.at[step],
            dst_ref=base_in.at[step],
            send_sem=base_send.at[step],
            recv_sem=base_recv.at[step],
            device_id=(host, other),
            device_id_type=MESH,
        )

    def send_base(step, carry):
        other = lax.rem(lane + step, n_tp)
        base_out[pl.ds(step, 1)] = project(other).astype(BF)[None]
        base_copy(other, step).start()
        return carry

    lax.fori_loop(1, n_tp, send_base, 0)
    own_base = project(lane)

    def wait_table(step, carry):
        table_copy(lax.rem(host + step, n_hst), host, step).wait()
        return carry

    lax.fori_loop(1, n_hst, wait_table, 0)
    table = tables[...]
    owned = jnp.right_shift(table, 5) == host
    ahead = dot(
        jnp.where(owned, 1.0, 0.0).astype(BF), jnp.where(s_sub < s_lane, 1.0, 0.0).astype(BF)
    )
    local_index = jnp.bitwise_and(table, 31).astype(F32)

    def place_index(place):
        got = jnp.where(owned & (ahead == place), local_index, -1.0)
        return jnp.broadcast_to(jnp.max(got, axis=1, keepdims=True), got.shape).astype(BF)

    spread_host = jnp.where(
        iota((send_total, n_hst), 0) // 8 == iota((send_total, n_hst), 1), 1.0, 0.0
    ).astype(BF)
    x_sub, x_lane = iota((send_total, 128), 0), iota((send_total, 128), 1)
    adapter = jnp.where(
        lax.rem(x_sub, 8) < 4,
        dot(spread_host, place_index(0.0)),
        dot(spread_host, place_index(1.0)),
    ) - jnp.where(x_lane >= 64, 1.0, 0.0)

    load_down.wait()

    def wait_rows(step, carry):
        block_copy(
            rows_out, rows_in, rows_send, rows_recv, lax.rem(host + step, n_hst), host, step
        ).wait()
        return carry

    lax.fori_loop(1, n_hst, wait_rows, 0)
    x_lo, x_hi = unpack(rows_in[...])
    owned_total, rank, _ = down_ref.shape
    pairs = owned_total // 2
    folded = jnp.zeros((send_total, 128), F32)
    for c in range(0, pairs, 2):
        d = down_ref[2 * c : 2 * c + 4].reshape(4 * rank, 2 * half)
        s = dot(x_lo, d[:, :half], NT) + dot(x_hi, d[:, half:], NT)
        folded = folded + jnp.where(adapter == 2.0 * c, s[:, :128], 0.0)
        folded = folded + jnp.where(adapter == 2.0 * c + 2.0, s[:, 128:], 0.0)
    folded = folded + pltpu.roll(folded, 64, 1)
    both = send_total // 2
    low_half = iota((both, 128), 1) < 64
    part_out[...] = jnp.where(low_half, folded[:both], folded[both:]).reshape(part_out.shape)

    def part_copy(other, step):
        return pltpu.make_async_remote_copy(
            src_ref=part_out.at[other],
            dst_ref=part_in.at[step],
            send_sem=part_send.at[step],
            recv_sem=part_recv.at[step],
            device_id=(host, other),
            device_id_type=MESH,
        )

    def send_part(step, carry):
        part_copy(lax.rem(lane + step, n_tp), step).start()
        return carry

    lax.fori_loop(1, n_tp, send_part, 0)

    def wait_base(step, carry):
        base_copy(lax.rem(lane + step, n_tp), step).wait()
        return carry

    lax.fori_loop(1, n_tp, wait_base, 0)
    base = own_base
    for step in range(1, n_tp):
        base = base + base_in[step].astype(F32)
    out_ref[...] = base

    def wait_part(step, carry):
        part_copy(lax.rem(lane + step, n_tp), step).wait()
        return carry

    lax.fori_loop(1, n_tp, wait_part, 0)
    total = part_out[lane]
    for step in range(1, n_tp):
        total = total + part_in[step]
    shrunk[pl.ds(lane, 1)] = total.astype(BF)[None]

    def shrunk_copy(other, step):
        return pltpu.make_async_remote_copy(
            src_ref=shrunk.at[lane],
            dst_ref=shrunk.at[lane],
            send_sem=shrunk_send.at[step],
            recv_sem=shrunk_recv.at[step],
            device_id=(host, other),
            device_id_type=MESH,
        )

    def send_shrunk(step, carry):
        shrunk_copy(lax.rem(lane + step, n_tp), step).start()
        return carry

    def wait_shrunk(step, carry):
        shrunk_copy(lax.rem(lane + step, n_tp), step).wait()
        return carry

    lax.fori_loop(1, n_tp, send_shrunk, 0)
    load_up.wait()
    lax.fori_loop(1, n_tp, wait_shrunk, 0)

    g = shrunk[...].reshape(both, 128).astype(F32)
    turned = pltpu.roll(g, 64, 1)
    full = jnp.concatenate(
        [jnp.where(low_half, g, turned), jnp.where(low_half, turned, g)], axis=0
    )
    raised = jnp.zeros((send_total, 2 * half), F32)
    for c in range(0, pairs, 2):
        e = jnp.concatenate(
            [
                jnp.where(adapter == 2.0 * c, full, 0.0),
                jnp.where(adapter == 2.0 * c + 2.0, full, 0.0),
            ],
            axis=1,
        ).astype(BF)
        raised = raised + dot(e, up_ref[2 * c : 2 * c + 4].reshape(4 * rank, 2 * half))
    back_out[...] = pack(raised[:, :half], raised[:, half:])

    def send_back(step, carry):
        block_copy(
            back_out, back_in, back_send, back_recv, lax.rem(host + step, n_hst), host, step
        ).start()
        return carry

    def wait_back(step, carry):
        block_copy(
            back_out, back_in, back_send, back_recv, lax.rem(host + step, n_hst), host, step
        ).wait()
        return carry

    lax.fori_loop(1, n_hst, send_back, 0)
    back_in[pl.ds(host, 1)] = back_out[pl.ds(host, 1)]
    lax.fori_loop(1, n_hst, wait_back, 0)
    y = back_in[...].reshape(n_hst * 16, half)
    out_ref[:, :half] += ADAPTER_SCALE * dot(gather_lo, y)
    out_ref[:, half:] += ADAPTER_SCALE * dot(gather_hi, y)


def local(
    queries,
    key_page_cache,
    value_page_cache,
    request_pages,
    context_length,
    output_weight,
    adapter_down_weight,
    adapter_up_weight,
    residual,
    host_slot_adapter,
    request_slot,
):
    n_hst, n_tp = lax.axis_size("hst"), lax.axis_size("tp")
    rows, width = queries.shape
    any_spec = pl.BlockSpec(memory_space=pl.ANY)
    smem = pl.BlockSpec(memory_space=pltpu.SMEM)
    vmem = pl.BlockSpec(memory_space=pltpu.VMEM)
    dma = pltpu.SemaphoreType.DMA
    block = (n_hst, 16, width // 2)
    part_rows = n_hst * 8 // 2 // n_tp
    summed = pl.pallas_call(
        functools.partial(kernel, n_hst, n_tp),
        out_shape=jax.ShapeDtypeStruct((rows, width), F32),
        in_specs=[any_spec, any_spec, any_spec, smem, smem, any_spec, any_spec, any_spec, vmem, vmem],
        out_specs=vmem,
        scratch_shapes=[
            pltpu.VMEM(queries.shape, BF),
            pltpu.VMEM(key_page_cache.shape, BF),
            pltpu.VMEM(value_page_cache.shape, BF),
            pltpu.VMEM(output_weight.shape, BF),
            pltpu.VMEM(adapter_down_weight.shape, BF),
            pltpu.VMEM(adapter_up_weight.shape, BF),
            pltpu.VMEM(queries.shape, BF),
            pltpu.VMEM((8, 128), jnp.int32),
            pltpu.VMEM((n_hst, 128), jnp.int32),
            pltpu.VMEM(block, BF),
            pltpu.VMEM(block, BF),
            pltpu.VMEM(block, BF),
            pltpu.VMEM(block, BF),
            pltpu.VMEM((n_tp, rows, width), BF),
            pltpu.VMEM((n_tp, rows, width), BF),
            pltpu.VMEM((n_tp, part_rows, 128), F32),
            pltpu.VMEM((n_tp, part_rows, 128), F32),
            pltpu.VMEM((n_tp, part_rows, 128), BF),
            dma((6,)),
            dma((n_hst,)),
            dma((n_hst,)),
            dma((n_hst,)),
            dma((n_hst,)),
            dma((n_hst,)),
            dma((n_hst,)),
            dma((n_tp,)),
            dma((n_tp,)),
            dma((n_tp,)),
            dma((n_tp,)),
            dma((n_tp,)),
            dma((n_tp,)),
        ],
        compiler_params=pltpu.CompilerParams(
            collective_id=0, has_side_effects=True, vmem_limit_bytes=48 * 1024 * 1024
        ),
        cost_estimate=pl.CostEstimate(
            flops=2_000_000_000, bytes_accessed=12_000_000, transcendentals=32768
        ),
        name="decode_step",
    )(
        queries,
        key_page_cache,
        value_page_cache,
        request_pages,
        context_length,
        output_weight,
        adapter_down_weight,
        adapter_up_weight,
        host_slot_adapter.reshape(1, -1),
        request_slot,
    )
    return (residual.astype(F32) + summed).astype(BF)


def solution(mesh):
    in_specs = (
        P("hst", "tp"),
        P("hst", None, "tp"),
        P("hst", None, "tp"),
        P("hst", None),
        P("hst"),
        P("tp", None),
        P("hst", None, "tp"),
        P("hst", None, "tp"),
        P("hst", "tp"),
        P("hst"),
        P("hst", None),
    )
    out_specs = P("hst", "tp")
    return jax.shard_map(local, mesh=mesh, in_specs=in_specs, out_specs=out_specs, check_vma=False)
```

```python
import functools
import math

import jax
import jax.numpy as jnp
from jax import lax
from jax.experimental import pallas as pl
from jax.experimental.pallas import tpu as pltpu
from jax.sharding import PartitionSpec as P

HD = 128
ADAPTER_SCALE = 2.0
Z, X = 8, 4
GROUPS = 2
MESH = pl.DeviceIdType.MESH
BF = jnp.bfloat16
F32 = jnp.float32
NT = (((1,), (1,)), ((), ()))
NN = (((1,), (0,)), ((), ()))


def dot(a, b, dims=NN):
    return lax.dot_general(a, b, dims, preferred_element_type=F32)


def iota(shape, dim):
    return lax.broadcasted_iota(jnp.int32, shape, dim)


def offsets(step):
    i, j = step // X, lax.rem(step, X)
    dz = Z // 2 + (1 - 2 * lax.rem(i, 2)) * ((i + 1) // 2)
    dx = X // 2 + (1 - 2 * lax.rem(j, 2)) * ((j + 1) // 2)
    return dz, dx


def ahead_of(host, step):
    dz, dx = offsets(step)
    return lax.rem(host // X + dz, Z) * X + lax.rem(lax.rem(host, X) + dx, X)


def behind(host, step):
    dz, dx = offsets(step)
    return lax.rem(host // X + Z - dz, Z) * X + lax.rem(lax.rem(host, X) + X - dx, X)


def kernel(
    n_hst,
    n_tp,
    q_hbm,
    k_hbm,
    v_hbm,
    pages_hbm,
    length_hbm,
    w_hbm,
    down_hbm,
    up_hbm,
    table_hbm,
    slot_hbm,
    out_ref,
    pages_ref,
    length_ref,
    table_ref,
    slot_ref,
    q_ref,
    k_ref,
    v_ref,
    w_ref,
    down_ref,
    up_ref,
    att_ref,
    table_out,
    tables,
    rows_out,
    rows_in,
    back_out,
    back_in,
    base_out,
    base_in,
    part_out,
    part_in,
    local_sem,
    table_send,
    table_recv,
    rows_send,
    rows_recv,
    back_send,
    back_recv,
    base_send,
    base_recv,
    part_send,
    part_recv,
):
    host = lax.axis_index("hst")
    lane = lax.axis_index("tp")

    def load(src, dst, i):
        return pltpu.make_async_copy(src, dst, local_sem.at[i])

    load_table = load(table_hbm, table_ref, 0)
    load_slot = load(slot_hbm, slot_ref, 1)
    load_pages = load(pages_hbm, pages_ref, 2)
    load_length = load(length_hbm, length_ref, 3)
    load_q = load(q_hbm, q_ref, 4)
    load_k = load(k_hbm, k_ref, 5)
    load_v = load(v_hbm, v_ref, 6)
    load_w = load(w_hbm, w_ref, 7)
    load_down = load(down_hbm, down_ref, 8)
    load_up = load(up_hbm, up_ref, 9)
    load_pages.start()
    load_length.start()
    load_table.start()
    load_slot.start()
    load_q.start()
    load_k.start()
    load_v.start()

    barrier = pltpu.get_barrier_semaphore()

    def greet_hosts(step, carry):
        other = ahead_of(host, step)
        pl.semaphore_signal(barrier, inc=1, device_id=(other, lane), device_id_type=MESH)
        return carry

    def greet_lanes(step, carry):
        other = lax.rem(lane + step, n_tp)
        pl.semaphore_signal(barrier, inc=1, device_id=(host, other), device_id_type=MESH)
        return carry

    lax.fori_loop(0, n_hst - 1, greet_hosts, 0)
    lax.fori_loop(1, n_tp, greet_lanes, 0)

    slots = table_ref.shape[1]
    row_total = slot_ref.shape[1]
    load_table.wait()
    load_slot.wait()
    table_out[...] = jnp.full(table_out.shape, -1, jnp.int32)
    table_out[0:1, 0:slots] = table_ref[...]
    table_row = table_out[0:1, :]
    owner_row = jnp.right_shift(table_row, 5)
    owner_all = jnp.broadcast_to(owner_row, (128, 128))
    s_sub, s_lane = iota((128, 128), 0), iota((128, 128), 1)
    owner_col = jnp.sum(jnp.where(s_sub == s_lane, owner_all, 0), axis=1, keepdims=True)
    place_row = jnp.sum(
        jnp.where((owner_col == owner_all) & (s_sub < s_lane), 1, 0), axis=0, keepdims=True
    )
    start_row = owner_row * 8 + place_row * 4
    chosen_row = slot_ref[...]
    r_sub, r_lane = iota((row_total, 128), 0), iota((row_total, 128), 1)
    q_sub, q_lane = iota((row_total, row_total), 0), iota((row_total, row_total), 1)
    chosen_col = jnp.sum(jnp.where(q_sub == q_lane, chosen_row, 0), axis=1, keepdims=True)
    before_col = jnp.sum(
        jnp.where((chosen_col == chosen_row) & (q_lane < q_sub), 1, 0), axis=1, keepdims=True
    )
    target_col = before_col + jnp.sum(
        jnp.where(chosen_col == r_lane, start_row, 0), axis=1, keepdims=True
    )
    target_row = jnp.sum(jnp.where(r_sub == r_lane, target_col, 0), axis=0, keepdims=True)
    send_total = n_hst * 8
    scatter = jnp.where(
        iota((send_total, row_total), 0) == target_row[:, :row_total], 1.0, 0.0
    ).astype(BF)
    back_place = (target_col // 8) * 16 + lax.rem(target_col, 8)
    back_lane = iota((row_total, n_hst * 16), 1)
    gather_lo = jnp.where(back_lane == back_place, 1.0, 0.0).astype(BF)
    gather_hi = jnp.where(back_lane == back_place + 8, 1.0, 0.0).astype(BF)

    load_pages.wait()
    load_length.wait()
    load_q.wait()
    load_k.wait()
    load_w.start()
    load_down.start()
    load_up.start()
    load_v.wait()
    heads = q_ref.shape[1] // HD
    tall = heads * 16
    member = lax.rem(iota((tall, HD), 0), 16)
    token = iota((tall, HD), 1)
    scale = 1.0 / math.sqrt(HD)

    def pages_of(ref, row):
        return [ref[pages_ref[p, row]] for p in range(pages_ref.shape[0])]

    def attend(group, carry):
        first = pl.multiple_of(group * 16, 16)
        q = q_ref[pl.ds(first, 16), :]
        q = jnp.concatenate([q[:, j * HD : (j + 1) * HD] for j in range(heads)], axis=0)
        logits = jnp.full((tall, HD), -jnp.inf, F32)
        for r in range(0, 16, 2):
            keys = jnp.concatenate(pages_of(k_ref, first + r) + pages_of(k_ref, first + r + 1), axis=0)
            s = dot(q, keys, NT)
            for i in range(2):
                live = (member == r + i) & (token < length_ref[first + r + i])
                logits = jnp.where(live, s[:, i * HD : (i + 1) * HD] * scale, logits)
        top = jnp.max(logits, axis=1, keepdims=True)
        e = jnp.exp(logits - top)
        p = e / jnp.sum(e, axis=1, keepdims=True)
        acc = jnp.zeros((tall, HD), F32)
        for r in range(0, 16, 2):
            values = jnp.concatenate(pages_of(v_ref, first + r) + pages_of(v_ref, first + r + 1), axis=0)
            spread = jnp.concatenate([jnp.where(member == r + i, p, 0.0) for i in range(2)], axis=1)
            acc = acc + dot(spread.astype(BF), values)
        acc = acc.astype(BF)
        for j in range(heads):
            att_ref[pl.ds(first, 16), j * HD : (j + 1) * HD] = acc[j * 16 : (j + 1) * 16]
        return carry

    lax.fori_loop(0, row_total // 32, attend, 0)

    pl.semaphore_wait(barrier, n_hst - 1 + n_tp - 1)
    tables[pl.ds(host, 1), :] = table_row

    def table_copy(step):
        return pltpu.make_async_remote_copy(
            src_ref=table_out.at[0:1, :],
            dst_ref=tables.at[pl.ds(host, 1), :],
            send_sem=table_send.at[step],
            recv_sem=table_recv.at[step],
            device_id=(ahead_of(host, step), lane),
            device_id_type=MESH,
        )

    def send_table(step, carry):
        table_copy(step).start()
        return carry

    lax.fori_loop(0, n_hst - 1, send_table, 0)
    lax.fori_loop(row_total // 32, row_total // 16, attend, 0)

    att = att_ref[...]
    half = att.shape[1] // 2

    def pack(lo, hi):
        blocks = lo.shape[0] // 8
        return jnp.concatenate(
            [lo.reshape(blocks, 8, half), hi.reshape(blocks, 8, half)], axis=1
        ).astype(BF)

    def unpack(x):
        rows = x.shape[0] * 8
        x = x.astype(F32)
        return x[:, :8].reshape(rows, half).astype(BF), x[:, 8:].reshape(rows, half).astype(BF)

    rows_out[...] = pack(dot(scatter, att[:, :half]), dot(scatter, att[:, half:]))

    def rows_copy(step):
        other = ahead_of(host, step)
        return pltpu.make_async_remote_copy(
            src_ref=rows_out.at[other],
            dst_ref=rows_in.at[step],
            send_sem=rows_send.at[step],
            recv_sem=rows_recv.at[step],
            device_id=(other, lane),
            device_id_type=MESH,
        )

    def send_rows(step, carry):
        rows_copy(step).start()
        return carry

    lax.fori_loop(0, n_hst - 1, send_rows, 0)
    rows_in[n_hst - 1 : n_hst] = rows_out[pl.ds(host, 1)]

    load_w.wait()
    width = out_ref.shape[1]

    def project(which):
        return dot(att, w_ref[:, pl.ds(pl.multiple_of(which * width, width), width)])

    def base_copy(step):
        return pltpu.make_async_remote_copy(
            src_ref=base_out.at[step],
            dst_ref=base_in.at[step],
            send_sem=base_send.at[step],
            recv_sem=base_recv.at[step],
            device_id=(host, lax.rem(lane + step, n_tp)),
            device_id_type=MESH,
        )

    def send_base(step, carry):
        base_out[pl.ds(step, 1)] = project(lax.rem(lane + step, n_tp)).astype(BF)[None]
        base_copy(step).start()
        return carry

    lax.fori_loop(1, n_tp, send_base, 0)
    out_ref[...] = project(lane)

    def wait_table(step, carry):
        table_copy(step).wait()
        return carry

    lax.fori_loop(0, n_hst - 1, wait_table, 0)
    table = tables[...]
    owned = jnp.right_shift(table, 5) == host
    ahead = dot(
        jnp.where(owned, 1.0, 0.0).astype(BF), jnp.where(s_sub < s_lane, 1.0, 0.0).astype(BF)
    )
    local_index = jnp.bitwise_and(table, 31).astype(F32)

    def place_index(place):
        got = jnp.where(owned & (ahead == place), local_index, -1.0)
        return jnp.broadcast_to(jnp.max(got, axis=1, keepdims=True), got.shape).astype(BF)

    group_hosts = n_hst // GROUPS
    group_rows = group_hosts * 8
    place_sub, place_lane = iota((group_rows, 128), 0), iota((group_rows, 128), 1)

    def adapters(group):
        step = group * group_hosts + iota((group_rows, n_hst), 0) // 8
        from_host = jnp.where(behind(host, step) == iota((group_rows, n_hst), 1), 1.0, 0.0).astype(BF)
        return jnp.where(
            lax.rem(place_sub, 8) < 4,
            dot(from_host, place_index(0.0)),
            dot(from_host, place_index(1.0)),
        ) - jnp.where(place_lane >= 64, 1.0, 0.0)

    adapter = [adapters(group) for group in range(GROUPS)]

    owned_total, rank, _ = down_ref.shape
    both = group_rows // 2
    low_half = iota((both, 128), 1) < 64

    def wait_rows(step, carry):
        rows_copy(step).wait()
        return carry

    def part_copy(group, step):
        return pltpu.make_async_remote_copy(
            src_ref=part_out.at[group],
            dst_ref=part_in.at[group * n_tp + step],
            send_sem=part_send.at[group * n_tp + step],
            recv_sem=part_recv.at[group * n_tp + step],
            device_id=(host, lax.rem(lane + step, n_tp)),
            device_id_type=MESH,
        )

    load_down.wait()
    own_part = []
    for group in range(GROUPS):
        first = group * group_hosts
        lax.fori_loop(first, min(first + group_hosts, n_hst - 1), wait_rows, 0)
        x_lo, x_hi = unpack(rows_in[first : first + group_hosts])
        folded = jnp.zeros((group_rows, 128), F32)
        for c in range(0, owned_total, 4):
            d = down_ref[c : c + 4].reshape(4 * rank, 2 * half)
            s = dot(x_lo, d[:, :half], NT) + dot(x_hi, d[:, half:], NT)
            folded = folded + jnp.where(adapter[group] == float(c), s[:, :128], 0.0)
            folded = folded + jnp.where(adapter[group] == float(c + 2), s[:, 128:], 0.0)
        folded = folded + pltpu.roll(folded, 64, 1)
        part = jnp.where(low_half, folded[:both], folded[both:])
        own_part.append(part)
        part_out[group] = part.astype(BF)

        def send_part(step, carry, group=group):
            part_copy(group, step).start()
            return carry

        lax.fori_loop(1, n_tp, send_part, 0)

    def wait_base(step, carry):
        base_copy(step).wait()
        return carry

    lax.fori_loop(1, n_tp, wait_base, 0)
    base = out_ref[...]
    for step in range(1, n_tp):
        base = base + base_in[step].astype(F32)
    out_ref[...] = base

    def back_copy(step):
        other = behind(host, step)
        return pltpu.make_async_remote_copy(
            src_ref=back_out.at[step],
            dst_ref=back_in.at[host],
            send_sem=back_send.at[step],
            recv_sem=back_recv.at[step],
            device_id=(other, lane),
            device_id_type=MESH,
        )

    def send_back(step, carry):
        back_copy(step).start()
        return carry

    def wait_back(step, carry):
        back_copy(step).wait()
        return carry

    load_up.wait()
    for group in range(GROUPS):

        def wait_part(step, carry, group=group):
            part_copy(group, step).wait()
            return carry

        lax.fori_loop(1, n_tp, wait_part, 0)
        g = own_part[group]
        for step in range(1, n_tp):
            g = g + part_in[group * n_tp + step].astype(F32)
        turned = pltpu.roll(g, 64, 1)
        full = jnp.concatenate(
            [jnp.where(low_half, g, turned), jnp.where(low_half, turned, g)], axis=0
        )
        raised = jnp.zeros((group_rows, 2 * half), F32)
        for c in range(0, owned_total, 4):
            e = jnp.concatenate(
                [
                    jnp.where(adapter[group] == float(c), full, 0.0),
                    jnp.where(adapter[group] == float(c + 2), full, 0.0),
                ],
                axis=1,
            ).astype(BF)
            raised = raised + dot(e, up_ref[c : c + 4].reshape(4 * rank, 2 * half))
        first = group * group_hosts
        back_out[first : first + group_hosts] = pack(raised[:, :half], raised[:, half:])
        lax.fori_loop(first, min(first + group_hosts, n_hst - 1), send_back, 0)

    back_in[pl.ds(host, 1)] = back_out[n_hst - 1 : n_hst]
    lax.fori_loop(0, n_hst - 1, wait_back, 0)
    y = back_in[...].reshape(n_hst * 16, half)
    out_ref[:, :half] += ADAPTER_SCALE * dot(gather_lo, y)
    out_ref[:, half:] += ADAPTER_SCALE * dot(gather_hi, y)


def local(
    queries,
    key_page_cache,
    value_page_cache,
    request_pages,
    context_length,
    output_weight,
    adapter_down_weight,
    adapter_up_weight,
    residual,
    host_slot_adapter,
    request_slot,
):
    n_hst, n_tp = lax.axis_size("hst"), lax.axis_size("tp")
    rows, width = queries.shape
    any_spec = pl.BlockSpec(memory_space=pl.ANY)
    dma = pltpu.SemaphoreType.DMA
    block = (n_hst, 16, width // 2)
    part_rows = n_hst * 8 // GROUPS // 2
    arguments = (
        queries,
        key_page_cache,
        value_page_cache,
        request_pages.T,
        context_length,
        output_weight,
        adapter_down_weight,
        adapter_up_weight,
        host_slot_adapter.reshape(1, -1),
        request_slot.T,
    )
    summed = pl.pallas_call(
        functools.partial(kernel, n_hst, n_tp),
        out_shape=jax.ShapeDtypeStruct((rows, width), F32),
        in_specs=[any_spec] * len(arguments),
        out_specs=pl.BlockSpec(memory_space=pltpu.VMEM),
        scratch_shapes=[
            pltpu.SMEM(request_pages.shape[::-1], jnp.int32),
            pltpu.SMEM(context_length.shape, jnp.int32),
            pltpu.VMEM((1, host_slot_adapter.shape[0]), jnp.int32),
            pltpu.VMEM((1, rows), jnp.int32),
            pltpu.VMEM(queries.shape, BF),
            pltpu.VMEM(key_page_cache.shape, BF),
            pltpu.VMEM(value_page_cache.shape, BF),
            pltpu.VMEM(output_weight.shape, BF),
            pltpu.VMEM(adapter_down_weight.shape, BF),
            pltpu.VMEM(adapter_up_weight.shape, BF),
            pltpu.VMEM(queries.shape, BF),
            pltpu.VMEM((8, 128), jnp.int32),
            pltpu.VMEM((n_hst, 128), jnp.int32),
            pltpu.VMEM(block, BF),
            pltpu.VMEM(block, BF),
            pltpu.VMEM(block, BF),
            pltpu.VMEM(block, BF),
            pltpu.VMEM((n_tp, rows, width), BF),
            pltpu.VMEM((n_tp, rows, width), BF),
            pltpu.VMEM((GROUPS, part_rows, 128), BF),
            pltpu.VMEM((GROUPS * n_tp, part_rows, 128), BF),
            dma((10,)),
            dma((n_hst,)),
            dma((n_hst,)),
            dma((n_hst,)),
            dma((n_hst,)),
            dma((n_hst,)),
            dma((n_hst,)),
            dma((n_tp,)),
            dma((n_tp,)),
            dma((GROUPS * n_tp,)),
            dma((GROUPS * n_tp,)),
        ],
        compiler_params=pltpu.CompilerParams(
            collective_id=0, has_side_effects=True, vmem_limit_bytes=40 * 1024 * 1024
        ),
        cost_estimate=pl.CostEstimate(
            flops=2_000_000_000, bytes_accessed=12_000_000, transcendentals=32768
        ),
        name="decode_step",
    )(*(pltpu.with_memory_space_constraint(a, pltpu.HBM) for a in arguments))
    return (residual.astype(F32) + summed).astype(BF)


def solution(mesh):
    in_specs = (
        P("hst", "tp"),
        P("hst", None, "tp"),
        P("hst", None, "tp"),
        P("hst", None),
        P("hst"),
        P("tp", None),
        P("hst", None, "tp"),
        P("hst", None, "tp"),
        P("hst", "tp"),
        P("hst"),
        P("hst", None),
    )
    out_specs = P("hst", "tp")
    return jax.shard_map(local, mesh=mesh, in_specs=in_specs, out_specs=out_specs, check_vma=False)
```

```python
import functools
import math

import jax
import jax.numpy as jnp
from jax import lax
from jax.experimental import pallas as pl
from jax.experimental.pallas import tpu as pltpu
from jax.sharding import PartitionSpec as P

HD = 128
ADAPTER_SCALE = 2.0
Z, X = 8, 4
GROUPS = 2
MESH = pl.DeviceIdType.MESH
BF = jnp.bfloat16
F32 = jnp.float32
NT = (((1,), (1,)), ((), ()))
NN = (((1,), (0,)), ((), ()))


def dot(a, b, dims=NN):
    return lax.dot_general(a, b, dims, preferred_element_type=F32)


def iota(shape, dim):
    return lax.broadcasted_iota(jnp.int32, shape, dim)


def offsets(step):
    i, j = step // X, lax.rem(step, X)
    dz = Z // 2 + (1 - 2 * lax.rem(i, 2)) * ((i + 1) // 2)
    dx = X // 2 + (1 - 2 * lax.rem(j, 2)) * ((j + 1) // 2)
    return dz, dx


def ahead_of(host, step):
    dz, dx = offsets(step)
    return lax.rem(host // X + dz, Z) * X + lax.rem(lax.rem(host, X) + dx, X)


def behind(host, step):
    dz, dx = offsets(step)
    return lax.rem(host // X + Z - dz, Z) * X + lax.rem(lax.rem(host, X) + X - dx, X)


def kernel(
    n_hst,
    n_tp,
    q_hbm,
    k_hbm,
    v_hbm,
    pages_hbm,
    length_hbm,
    w_hbm,
    down_hbm,
    up_hbm,
    table_hbm,
    slot_hbm,
    out_ref,
    pages_ref,
    length_ref,
    table_ref,
    slot_ref,
    q_ref,
    k_ref,
    v_ref,
    w_ref,
    down_ref,
    up_ref,
    att_ref,
    table_out,
    tables,
    rows_out,
    rows_in,
    back_out,
    back_in,
    pair_out,
    pair_in,
    base_own,
    base_out,
    base_in,
    part_out,
    part_in,
    local_sem,
    table_send,
    table_recv,
    rows_send,
    rows_recv,
    back_send,
    back_recv,
    pair_send,
    pair_recv,
    base_send,
    base_recv,
    part_send,
    part_recv,
):
    host = lax.axis_index("hst")
    lane = lax.axis_index("tp")

    def load(src, dst, i):
        return pltpu.make_async_copy(src, dst, local_sem.at[i])

    load_table = load(table_hbm, table_ref, 0)
    load_slot = load(slot_hbm, slot_ref, 1)
    load_pages = load(pages_hbm, pages_ref, 2)
    load_length = load(length_hbm, length_ref, 3)
    load_q = load(q_hbm, q_ref, 4)
    load_k = load(k_hbm, k_ref, 5)
    load_v = load(v_hbm, v_ref, 6)
    load_w = load(w_hbm, w_ref, 7)
    load_down = load(down_hbm, down_ref, 8)
    load_up = load(up_hbm, up_ref, 9)
    load_pages.start()
    load_q.start()
    load_k.start()
    load_length.start()
    load_table.start()
    load_slot.start()
    load_v.start()

    barrier = pltpu.get_barrier_semaphore()

    def greet_hosts(step, carry):
        other = ahead_of(host, step)
        pl.semaphore_signal(barrier, inc=1, device_id=(other, lane), device_id_type=MESH)
        return carry

    def greet_lanes(step, carry):
        other = lax.rem(lane + step, n_tp)
        pl.semaphore_signal(barrier, inc=1, device_id=(host, other), device_id_type=MESH)
        return carry

    lax.fori_loop(0, n_hst - 1, greet_hosts, 0)
    lax.fori_loop(1, n_tp, greet_lanes, 0)

    slots = table_ref.shape[1]
    row_total = slot_ref.shape[1]
    load_table.wait()
    load_slot.wait()
    table_out[...] = jnp.full(table_out.shape, -1, jnp.int32)
    table_out[0:1, 0:slots] = table_ref[...]
    table_row = table_out[0:1, :]
    owner_row = jnp.right_shift(table_row, 5)
    owner_all = jnp.broadcast_to(owner_row, (128, 128))
    s_sub, s_lane = iota((128, 128), 0), iota((128, 128), 1)
    owner_col = jnp.sum(jnp.where(s_sub == s_lane, owner_all, 0), axis=1, keepdims=True)
    place_row = jnp.sum(
        jnp.where((owner_col == owner_all) & (s_sub < s_lane), 1, 0), axis=0, keepdims=True
    )
    start_row = owner_row * 8 + place_row * 4
    chosen_row = slot_ref[...]
    r_sub, r_lane = iota((row_total, 128), 0), iota((row_total, 128), 1)
    q_sub, q_lane = iota((row_total, row_total), 0), iota((row_total, row_total), 1)
    chosen_col = jnp.sum(jnp.where(q_sub == q_lane, chosen_row, 0), axis=1, keepdims=True)
    before_col = jnp.sum(
        jnp.where((chosen_col == chosen_row) & (q_lane < q_sub), 1, 0), axis=1, keepdims=True
    )
    target_col = before_col + jnp.sum(
        jnp.where(chosen_col == r_lane, start_row, 0), axis=1, keepdims=True
    )
    target_row = jnp.sum(jnp.where(r_sub == r_lane, target_col, 0), axis=0, keepdims=True)
    send_total = n_hst * 8
    scatter = jnp.where(
        iota((send_total, row_total), 0) == target_row[:, :row_total], 1.0, 0.0
    ).astype(BF)
    back_place = (target_col // 8) * 16 + lax.rem(target_col, 8)
    back_lane = iota((row_total, n_hst * 16), 1)
    gather_lo = jnp.where(back_lane == back_place, 1.0, 0.0).astype(BF)
    gather_hi = jnp.where(back_lane == back_place + 8, 1.0, 0.0).astype(BF)

    load_pages.wait()
    load_length.wait()
    load_q.wait()
    load_k.wait()
    load_w.start()
    load_down.start()
    load_up.start()
    load_v.wait()
    heads = q_ref.shape[1] // HD
    tall = heads * 16
    member = lax.rem(iota((tall, HD), 0), 16)
    token = iota((tall, HD), 1)
    scale = 1.0 / math.sqrt(HD)

    def pages_of(ref, row):
        return [ref[pages_ref[p, row]] for p in range(pages_ref.shape[0])]

    def attend(group, carry):
        first = pl.multiple_of(group * 16, 16)
        q = q_ref[pl.ds(first, 16), :]
        q = jnp.concatenate([q[:, j * HD : (j + 1) * HD] for j in range(heads)], axis=0)
        logits = jnp.full((tall, HD), -jnp.inf, F32)
        for r in range(0, 16, 2):
            keys = jnp.concatenate(pages_of(k_ref, first + r) + pages_of(k_ref, first + r + 1), axis=0)
            s = dot(q, keys, NT)
            for i in range(2):
                live = (member == r + i) & (token < length_ref[first + r + i])
                logits = jnp.where(live, s[:, i * HD : (i + 1) * HD] * scale, logits)
        top = jnp.max(logits, axis=1, keepdims=True)
        e = jnp.exp(logits - top)
        p = e / jnp.sum(e, axis=1, keepdims=True)
        acc = jnp.zeros((tall, HD), F32)
        for r in range(0, 16, 2):
            values = jnp.concatenate(pages_of(v_ref, first + r) + pages_of(v_ref, first + r + 1), axis=0)
            spread = jnp.concatenate([jnp.where(member == r + i, p, 0.0) for i in range(2)], axis=1)
            acc = acc + dot(spread.astype(BF), values)
        acc = acc.astype(BF)
        for j in range(heads):
            att_ref[pl.ds(first, 16), j * HD : (j + 1) * HD] = acc[j * 16 : (j + 1) * 16]
        return carry

    lax.fori_loop(0, row_total // 16, attend, 0)

    att = att_ref[...]
    half = att.shape[1] // 2

    def pack(lo, hi):
        blocks = lo.shape[0] // 8
        return jnp.concatenate(
            [lo.reshape(blocks, 8, half), hi.reshape(blocks, 8, half)], axis=1
        ).astype(BF)

    def unpack(x):
        rows = x.shape[0] * 8
        x = x.astype(F32)
        return x[:, :8].reshape(rows, half).astype(BF), x[:, 8:].reshape(rows, half).astype(BF)

    rows_out[...] = pack(dot(scatter, att[:, :half]), dot(scatter, att[:, half:]))

    def arrived(ref, sem):
        pltpu.make_async_copy(ref, ref, sem).wait()

    def table_copy(step):
        return pltpu.make_async_remote_copy(
            src_ref=table_out.at[0:1, :],
            dst_ref=tables.at[pl.ds(host, 1), :],
            send_sem=table_send,
            recv_sem=table_recv,
            device_id=(ahead_of(host, step), lane),
            device_id_type=MESH,
        )

    def rows_copy(step, group):
        other = ahead_of(host, step)
        return pltpu.make_async_remote_copy(
            src_ref=rows_out.at[other],
            dst_ref=rows_in.at[step],
            send_sem=rows_send,
            recv_sem=rows_recv.at[group],
            device_id=(other, lane),
            device_id_type=MESH,
        )

    group_hosts = n_hst // GROUPS
    last = n_hst - 1

    pl.semaphore_wait(barrier, n_hst - 1 + n_tp - 1)
    for group in range(GROUPS):

        def send_rows(step, carry, group=group):
            table_copy(step).start()
            rows_copy(step, group).start()
            return carry

        first = group * group_hosts
        lax.fori_loop(first, min(first + group_hosts, last), send_rows, 0)
    pltpu.make_async_copy(table_out.at[0:1, :], tables.at[pl.ds(host, 1), :], table_recv).start()
    pltpu.make_async_copy(rows_out.at[host], rows_in.at[last], rows_recv.at[GROUPS - 1]).start()

    load_w.wait()
    width = out_ref.shape[1]
    chips = n_tp // 2
    chip, core = lane // 2, lax.rem(lane, 2)
    turns = (2, 1, 3, 0)

    def project(which):
        return dot(att, w_ref[:, pl.ds(pl.multiple_of(which * width, width), width)])

    def chip_at(turn):
        return lax.rem(chip + turn, chips)

    def pair_copy():
        return pltpu.make_async_remote_copy(
            src_ref=pair_out,
            dst_ref=pair_in,
            send_sem=pair_send,
            recv_sem=pair_recv,
            device_id=(host, lane + 1 - 2 * core),
            device_id_type=MESH,
        )

    def base_copy(i):
        return pltpu.make_async_remote_copy(
            src_ref=base_out.at[i],
            dst_ref=base_in.at[i],
            send_sem=base_send,
            recv_sem=base_recv,
            device_id=(host, 2 * chip_at(turns[i]) + core),
            device_id_type=MESH,
        )

    for i, turn in enumerate(turns):
        pair_out[i] = project(2 * chip_at(turn) + 1 - core).astype(BF)
    pair_copy().start()
    for i, turn in enumerate(turns):
        base_own[i] = project(2 * chip_at(turn) + core)
    pair_copy().wait()
    for i in range(chips - 1):
        base_out[i] = (base_own[i] + pair_in[i].astype(F32)).astype(BF)
        base_copy(i).start()
    out_ref[...] = base_own[chips - 1] + pair_in[chips - 1].astype(F32)

    arrived(tables, table_recv)
    table = tables[...]
    owned = jnp.right_shift(table, 5) == host
    ahead = dot(
        jnp.where(owned, 1.0, 0.0).astype(BF), jnp.where(s_sub < s_lane, 1.0, 0.0).astype(BF)
    )
    local_index = jnp.bitwise_and(table, 31).astype(F32)

    def place_index(place):
        got = jnp.where(owned & (ahead == place), local_index, -1.0)
        return jnp.broadcast_to(jnp.max(got, axis=1, keepdims=True), got.shape).astype(BF)

    group_rows = group_hosts * 8
    place_sub, place_lane = iota((group_rows, 128), 0), iota((group_rows, 128), 1)

    def adapters(group):
        step = group * group_hosts + iota((group_rows, n_hst), 0) // 8
        from_host = jnp.where(behind(host, step) == iota((group_rows, n_hst), 1), 1.0, 0.0).astype(BF)
        return jnp.where(
            lax.rem(place_sub, 8) < 4,
            dot(from_host, place_index(0.0)),
            dot(from_host, place_index(1.0)),
        ) - jnp.where(place_lane >= 64, 1.0, 0.0)

    adapter = [adapters(group) for group in range(GROUPS)]

    owned_total, rank, _ = down_ref.shape
    both = group_rows // 2
    low_half = iota((both, 128), 1) < 64

    def part_copy(group, step):
        return pltpu.make_async_remote_copy(
            src_ref=part_out.at[group],
            dst_ref=part_in.at[group, step - 1],
            send_sem=part_send,
            recv_sem=part_recv.at[group],
            device_id=(host, lax.rem(lane + step, n_tp)),
            device_id_type=MESH,
        )

    load_down.wait()
    own_part = []
    for group in range(GROUPS):
        first = group * group_hosts
        arrived(rows_in.at[first : first + group_hosts], rows_recv.at[group])
        x_lo, x_hi = unpack(rows_in[first : first + group_hosts])
        folded = jnp.zeros((group_rows, 128), F32)
        for c in range(0, owned_total, 4):
            d = down_ref[c : c + 4].reshape(4 * rank, 2 * half)
            s = dot(x_lo, d[:, :half], NT) + dot(x_hi, d[:, half:], NT)
            folded = folded + jnp.where(adapter[group] == float(c), s[:, :128], 0.0)
            folded = folded + jnp.where(adapter[group] == float(c + 2), s[:, 128:], 0.0)
        folded = folded + pltpu.roll(folded, 64, 1)
        part = jnp.where(low_half, folded[:both], folded[both:])
        own_part.append(part)
        part_out[group] = part.astype(BF)

        def send_part(step, carry, group=group):
            part_copy(group, step).start()
            return carry

        lax.fori_loop(1, n_tp, send_part, 0)

    arrived(base_in, base_recv)
    base = out_ref[...]
    for i in range(chips - 1):
        base = base + base_in[i].astype(F32)
    out_ref[...] = base

    def back_copy(step):
        other = behind(host, step)
        return pltpu.make_async_remote_copy(
            src_ref=back_out.at[step],
            dst_ref=back_in.at[host],
            send_sem=back_send,
            recv_sem=back_recv,
            device_id=(other, lane),
            device_id_type=MESH,
        )

    def send_back(step, carry):
        back_copy(step).start()
        return carry

    load_up.wait()
    for group in range(GROUPS):
        arrived(part_in.at[group], part_recv.at[group])
        g = own_part[group]
        for step in range(1, n_tp):
            g = g + part_in[group, step - 1].astype(F32)
        turned = pltpu.roll(g, 64, 1)
        full = jnp.concatenate(
            [jnp.where(low_half, g, turned), jnp.where(low_half, turned, g)], axis=0
        )
        raised = jnp.zeros((group_rows, 2 * half), F32)
        for c in range(0, owned_total, 4):
            e = jnp.concatenate(
                [
                    jnp.where(adapter[group] == float(c), full, 0.0),
                    jnp.where(adapter[group] == float(c + 2), full, 0.0),
                ],
                axis=1,
            ).astype(BF)
            raised = raised + dot(e, up_ref[c : c + 4].reshape(4 * rank, 2 * half))
        first = group * group_hosts
        back_out[first : first + group_hosts] = pack(raised[:, :half], raised[:, half:])
        lax.fori_loop(first, min(first + group_hosts, last), send_back, 0)

    pltpu.make_async_copy(back_out.at[last], back_in.at[host], back_recv).start()
    arrived(back_in, back_recv)
    y = back_in[...].reshape(n_hst * 16, half)
    out_ref[:, :half] += ADAPTER_SCALE * dot(gather_lo, y)
    out_ref[:, half:] += ADAPTER_SCALE * dot(gather_hi, y)

    arrived(tables.at[0:last], table_send)
    arrived(rows_out.at[0:last], rows_send)
    arrived(back_out.at[0:last], back_send)
    arrived(base_out, base_send)
    arrived(part_in, part_send)


def local(
    queries,
    key_page_cache,
    value_page_cache,
    request_pages,
    context_length,
    output_weight,
    adapter_down_weight,
    adapter_up_weight,
    residual,
    host_slot_adapter,
    request_slot,
):
    n_hst, n_tp = lax.axis_size("hst"), lax.axis_size("tp")
    rows, width = queries.shape
    any_spec = pl.BlockSpec(memory_space=pl.ANY)
    dma = pltpu.SemaphoreType.DMA
    block = (n_hst, 16, width // 2)
    part_rows = n_hst * 8 // GROUPS // 2
    arguments = (
        queries,
        key_page_cache,
        value_page_cache,
        request_pages.T,
        context_length,
        output_weight,
        adapter_down_weight,
        adapter_up_weight,
        host_slot_adapter.reshape(1, -1),
        request_slot.T,
    )
    summed = pl.pallas_call(
        functools.partial(kernel, n_hst, n_tp),
        out_shape=jax.ShapeDtypeStruct((rows, width), F32),
        in_specs=[any_spec] * len(arguments),
        out_specs=pl.BlockSpec(memory_space=pltpu.VMEM),
        scratch_shapes=[
            pltpu.SMEM(request_pages.shape[::-1], jnp.int32),
            pltpu.SMEM(context_length.shape, jnp.int32),
            pltpu.VMEM((1, host_slot_adapter.shape[0]), jnp.int32),
            pltpu.VMEM((1, rows), jnp.int32),
            pltpu.VMEM(queries.shape, BF),
            pltpu.VMEM(key_page_cache.shape, BF),
            pltpu.VMEM(value_page_cache.shape, BF),
            pltpu.VMEM(output_weight.shape, BF),
            pltpu.VMEM(adapter_down_weight.shape, BF),
            pltpu.VMEM(adapter_up_weight.shape, BF),
            pltpu.VMEM(queries.shape, BF),
            pltpu.VMEM((8, 128), jnp.int32),
            pltpu.VMEM((n_hst, 128), jnp.int32),
            pltpu.VMEM(block, BF),
            pltpu.VMEM(block, BF),
            pltpu.VMEM(block, BF),
            pltpu.VMEM(block, BF),
            pltpu.VMEM((n_tp // 2, rows, width), BF),
            pltpu.VMEM((n_tp // 2, rows, width), BF),
            pltpu.VMEM((n_tp // 2, rows, width), F32),
            pltpu.VMEM((n_tp // 2 - 1, rows, width), BF),
            pltpu.VMEM((n_tp // 2 - 1, rows, width), BF),
            pltpu.VMEM((GROUPS, part_rows, 128), BF),
            pltpu.VMEM((GROUPS, n_tp - 1, part_rows, 128), BF),
            dma((10,)),
            dma,
            dma,
            dma,
            dma((GROUPS,)),
            dma,
            dma,
            dma,
            dma,
            dma,
            dma,
            dma,
            dma((GROUPS,)),
        ],
        compiler_params=pltpu.CompilerParams(
            collective_id=0, has_side_effects=True, vmem_limit_bytes=40 * 1024 * 1024
        ),
        cost_estimate=pl.CostEstimate(
            flops=2_000_000_000, bytes_accessed=12_000_000, transcendentals=32768
        ),
        name="decode_step",
    )(*(pltpu.with_memory_space_constraint(a, pltpu.HBM) for a in arguments))
    return (residual.astype(F32) + summed).astype(BF)


def solution(mesh):
    in_specs = (
        P("hst", "tp"),
        P("hst", None, "tp"),
        P("hst", None, "tp"),
        P("hst", None),
        P("hst"),
        P("tp", None),
        P("hst", None, "tp"),
        P("hst", None, "tp"),
        P("hst", "tp"),
        P("hst"),
        P("hst", None),
    )
    out_specs = P("hst", "tp")
    return jax.shard_map(local, mesh=mesh, in_specs=in_specs, out_specs=out_specs, check_vma=False)
```

```python
import functools
import math

import jax
import jax.numpy as jnp
from jax import lax
from jax.experimental import pallas as pl
from jax.experimental.pallas import tpu as pltpu
from jax.sharding import PartitionSpec as P

HD = 128
ADAPTER_SCALE = 2.0
Z, X = 8, 4
GROUPS = 2
MESH = pl.DeviceIdType.MESH
BF = jnp.bfloat16
F32 = jnp.float32
NT = (((1,), (1,)), ((), ()))
NN = (((1,), (0,)), ((), ()))


def dot(a, b, dims=NN):
    return lax.dot_general(a, b, dims, preferred_element_type=F32)


def iota(shape, dim):
    return lax.broadcasted_iota(jnp.int32, shape, dim)


def offsets(step):
    i, j = step // X, step % X
    dz = Z // 2 + (1 - 2 * (i % 2)) * ((i + 1) // 2)
    dx = X // 2 + (1 - 2 * (j % 2)) * ((j + 1) // 2)
    return dz, dx


def ahead_of(host, step):
    dz, dx = offsets(step)
    return lax.rem(host // X + dz, Z) * X + lax.rem(lax.rem(host, X) + dx, X)


def behind(host, step):
    dz, dx = offsets(step)
    return lax.rem(host // X + Z - dz, Z) * X + lax.rem(lax.rem(host, X) + X - dx, X)


def kernel(
    n_hst,
    n_tp,
    q_hbm,
    k_hbm,
    v_hbm,
    pages_hbm,
    length_hbm,
    w_hbm,
    down_hbm,
    up_hbm,
    table_hbm,
    slot_hbm,
    out_ref,
    pages_ref,
    length_ref,
    table_ref,
    slot_ref,
    q_ref,
    logits_ref,
    k_ref,
    v_ref,
    w_ref,
    down_ref,
    up_ref,
    att_ref,
    table_out,
    tables,
    rows_out,
    rows_in,
    back_out,
    back_in,
    pair_out,
    pair_in,
    base_own,
    base_out,
    base_in,
    part_out,
    part_in,
    local_sem,
    table_send,
    table_recv,
    rows_send,
    rows_recv,
    back_send,
    back_recv,
    pair_send,
    pair_recv,
    base_send,
    base_recv,
    part_send,
    part_recv,
):
    host = lax.axis_index("hst")
    lane = lax.axis_index("tp")

    def load(src, dst, i):
        return pltpu.make_async_copy(src, dst, local_sem.at[i])

    load_table = load(table_hbm, table_ref, 0)
    load_slot = load(slot_hbm, slot_ref, 1)
    load_pages = load(pages_hbm, pages_ref, 2)
    load_length = load(length_hbm, length_ref, 3)
    load_q = load(q_hbm, q_ref, 4)
    load_k = load(k_hbm, k_ref, 5)
    load_v = load(v_hbm, v_ref, 6)
    load_w = load(w_hbm, w_ref, 7)
    load_down = load(down_hbm, down_ref, 8)
    load_up = load(up_hbm, up_ref, 9)
    load_pages.start()
    load_q.start()
    load_k.start()
    load_length.start()
    load_table.start()
    load_slot.start()
    load_v.start()

    barrier = pltpu.get_barrier_semaphore()

    def greet_hosts(step):
        other = ahead_of(host, step)
        pl.semaphore_signal(barrier, inc=1, device_id=(other, lane), device_id_type=MESH)

    def greet_lanes(step):
        other = lax.rem(lane + step, n_tp)
        pl.semaphore_signal(barrier, inc=1, device_id=(host, other), device_id_type=MESH)

    for step in range(n_hst - 1):
        greet_hosts(step)
    for step in range(1, n_tp):
        greet_lanes(step)

    slots = table_ref.shape[1]
    row_total = slot_ref.shape[1]
    load_table.wait()
    load_slot.wait()
    table_out[...] = jnp.full(table_out.shape, -1, jnp.int32)
    table_out[0:1, 0:slots] = table_ref[...]
    table_row = table_out[0:1, :]
    owner_row = jnp.right_shift(table_row, 5)
    owner_all = jnp.broadcast_to(owner_row, (128, 128))
    s_sub, s_lane = iota((128, 128), 0), iota((128, 128), 1)
    owner_col = jnp.sum(jnp.where(s_sub == s_lane, owner_all, 0), axis=1, keepdims=True)
    place_row = jnp.sum(
        jnp.where((owner_col == owner_all) & (s_sub < s_lane), 1, 0), axis=0, keepdims=True
    )
    start_row = owner_row * 8 + place_row * 4
    chosen_row = slot_ref[...]
    r_sub, r_lane = iota((row_total, 128), 0), iota((row_total, 128), 1)
    q_sub, q_lane = iota((row_total, row_total), 0), iota((row_total, row_total), 1)
    chosen_col = jnp.sum(jnp.where(q_sub == q_lane, chosen_row, 0), axis=1, keepdims=True)
    before_col = jnp.sum(
        jnp.where((chosen_col == chosen_row) & (q_lane < q_sub), 1, 0), axis=1, keepdims=True
    )
    target_col = before_col + jnp.sum(
        jnp.where(chosen_col == r_lane, start_row, 0), axis=1, keepdims=True
    )
    target_row = jnp.sum(jnp.where(r_sub == r_lane, target_col, 0), axis=0, keepdims=True)
    send_total = n_hst * 8
    scatter = jnp.where(
        iota((send_total, row_total), 0) == target_row[:, :row_total], 1.0, 0.0
    ).astype(BF)
    back_place = (target_col // 8) * 16 + lax.rem(target_col, 8)
    back_lane = iota((row_total, n_hst * 16), 1)
    gather_lo = jnp.where(back_lane == back_place, 1.0, 0.0).astype(BF)
    gather_hi = jnp.where(back_lane == back_place + 8, 1.0, 0.0).astype(BF)

    heads = q_ref.shape[1] // HD
    tall = heads * 8
    load_length.wait()
    row = iota((row_total * heads, row_total), 0)
    request = row // tall * 8 + lax.rem(row, 8)
    length_col = jnp.sum(
        jnp.where(iota(row.shape, 1) == request, length_ref[...], 0), axis=1, keepdims=True
    )

    load_pages.wait()
    load_q.wait()
    load_k.wait()
    load_w.start()
    load_down.start()
    load_up.start()
    sub = iota((8, HD), 0)

    def pages_of(ref, row):
        return [ref[pages_ref[p, row]] for p in range(pages_ref.shape[0])]

    def pair_of(ref, row):
        return jnp.concatenate(pages_of(ref, row) + pages_of(ref, row + 1), axis=0)

    def match(step, carry):
        first = pl.multiple_of(step * 16, 16)
        q16 = q_ref[pl.ds(first, 16), :].astype(F32)
        for part in range(2):
            q = q16[part * 8 : (part + 1) * 8]
            q = jnp.concatenate([q[:, j * HD : (j + 1) * HD] for j in range(heads)], axis=0).astype(BF)
            got = [jnp.zeros((8, HD), F32)] * heads
            for r in range(0, 8, 2):
                s = dot(q, pair_of(k_ref, first + part * 8 + r), NT)
                for j in range(heads):
                    rows8 = s[j * 8 : (j + 1) * 8]
                    got[j] = jnp.where(sub == r, rows8[:, :HD], got[j])
                    got[j] = jnp.where(sub == r + 1, rows8[:, HD:], got[j])
            logits_ref[pl.ds(pl.multiple_of((step * 2 + part) * tall, tall), tall), :] = jnp.concatenate(
                got, axis=0
            )
        return carry

    lax.fori_loop(0, row_total // 16, match, 0)

    live = iota((row_total * heads, HD), 1) < length_col
    logits = jnp.where(live, logits_ref[...] * (1.0 / math.sqrt(HD)), -jnp.inf)
    e = jnp.exp(logits - jnp.max(logits, axis=1, keepdims=True))
    logits_ref[...] = e / jnp.sum(e, axis=1, keepdims=True)

    load_v.wait()

    def blend(step, carry):
        first = pl.multiple_of(step * 16, 16)
        for part in range(2):
            p = logits_ref[pl.ds(pl.multiple_of((step * 2 + part) * tall, tall), tall), :]
            p = [p[j * 8 : (j + 1) * 8] for j in range(heads)]
            acc = jnp.zeros((tall, HD), F32)
            for r in range(0, 8, 2):
                spread = jnp.concatenate(
                    [
                        jnp.concatenate([jnp.where(sub == r + i, x, 0.0) for x in p], axis=0)
                        for i in range(2)
                    ],
                    axis=1,
                )
                acc = acc + dot(spread.astype(BF), pair_of(v_ref, first + part * 8 + r))
            for j in range(heads):
                att_ref[pl.ds(first + part * 8, 8), j * HD : (j + 1) * HD] = acc[j * 8 : (j + 1) * 8]
        return carry

    lax.fori_loop(0, row_total // 16, blend, 0)

    att = att_ref[...].astype(BF)
    half = att.shape[1] // 2

    def pack(lo, hi):
        blocks = lo.shape[0] // 8
        return jnp.concatenate(
            [lo.reshape(blocks, 8, half), hi.reshape(blocks, 8, half)], axis=1
        ).astype(BF)

    def unpack(x):
        rows = x.shape[0] * 8
        x = x.astype(F32)
        lo, hi = x[:, :8].reshape(rows, half), x[:, 8:].reshape(rows, half)
        return jnp.concatenate([lo, hi], axis=1).astype(BF)

    rows_out[...] = pack(dot(scatter, att[:, :half]), dot(scatter, att[:, half:]))

    def arrived(ref, sem):
        pltpu.make_async_copy(ref, ref, sem).wait()

    def table_copy(step, group):
        return pltpu.make_async_remote_copy(
            src_ref=table_out.at[0:1, :],
            dst_ref=tables.at[pl.ds(step, 1), :],
            send_sem=table_send,
            recv_sem=table_recv.at[group],
            device_id=(ahead_of(host, step), lane),
            device_id_type=MESH,
        )

    def rows_copy(step, group):
        other = ahead_of(host, step)
        return pltpu.make_async_remote_copy(
            src_ref=rows_out.at[other],
            dst_ref=rows_in.at[step],
            send_sem=rows_send,
            recv_sem=rows_recv.at[group],
            device_id=(other, lane),
            device_id_type=MESH,
        )

    group_hosts = n_hst // GROUPS
    last = n_hst - 1

    pl.semaphore_wait(barrier, n_hst - 1 + n_tp - 1)
    for group in reversed(range(GROUPS)):
        first = group * group_hosts
        for step in range(first, min(first + group_hosts, last)):
            table_copy(step, group).start()
            rows_copy(step, group).start()
    pltpu.make_async_copy(
        table_out.at[0:1, :], tables.at[last : last + 1, :], table_recv.at[GROUPS - 1]
    ).start()
    pltpu.make_async_copy(rows_out.at[host], rows_in.at[last], rows_recv.at[GROUPS - 1]).start()

    load_w.wait()
    width = out_ref.shape[1]
    chips = n_tp // 2
    chip, core = lane // 2, lax.rem(lane, 2)
    turns = (2, 1, 3, 0)

    def project(which):
        return dot(att, w_ref[:, pl.ds(pl.multiple_of(which * width, width), width)])

    def chip_at(turn):
        return lax.rem(chip + turn, chips)

    def pair_copy():
        return pltpu.make_async_remote_copy(
            src_ref=pair_out,
            dst_ref=pair_in,
            send_sem=pair_send,
            recv_sem=pair_recv,
            device_id=(host, lane + 1 - 2 * core),
            device_id_type=MESH,
        )

    def base_copy(i):
        return pltpu.make_async_remote_copy(
            src_ref=base_out.at[i],
            dst_ref=base_in.at[i],
            send_sem=base_send,
            recv_sem=base_recv,
            device_id=(host, 2 * chip_at(turns[i]) + core),
            device_id_type=MESH,
        )

    for i, turn in enumerate(turns):
        pair_out[i] = project(2 * chip_at(turn) + 1 - core).astype(BF)
    pair_copy().start()
    for i, turn in enumerate(turns):
        base_own[i] = project(2 * chip_at(turn) + core)
    pair_copy().wait()
    for i in range(chips - 1):
        base_out[i] = (base_own[i] + pair_in[i].astype(F32)).astype(BF)
        base_copy(i).start()
    out_ref[...] = base_own[chips - 1] + pair_in[chips - 1].astype(F32)

    group_rows = group_hosts * 8
    owned_total, rank, _ = down_ref.shape
    place_sub, place_lane = iota((group_rows, 128), 0), iota((group_rows, 128), 1)
    from_host = iota((group_rows, group_hosts), 0) // 8 == iota((group_rows, group_hosts), 1)
    from_host = jnp.where(from_host, 1.0, 0.0).astype(BF)
    earlier = jnp.where(s_sub < s_lane, 1.0, 0.0).astype(BF)

    def adapters(group):
        first = group * group_hosts
        table = tables[first : first + group_hosts]
        owned = jnp.right_shift(table, 5) == host
        ahead = dot(jnp.where(owned, 1.0, 0.0).astype(BF), earlier)
        local_index = jnp.bitwise_and(table, 31).astype(F32)

        def place_index(place):
            got = jnp.where(owned & (ahead == place), local_index, -1.0)
            got = jnp.broadcast_to(jnp.max(got, axis=1, keepdims=True), got.shape).astype(BF)
            return dot(from_host, got)

        found = jnp.where(lax.rem(place_sub, 8) < 4, place_index(0.0), place_index(1.0))
        return found - jnp.where(place_lane >= 64, 1.0, 0.0), found.T[:rank]


    def part_copy(group, step):
        return pltpu.make_async_remote_copy(
            src_ref=part_out.at[group],
            dst_ref=part_in.at[group, step - 1],
            send_sem=part_send,
            recv_sem=part_recv.at[group],
            device_id=(host, lax.rem(lane + step, n_tp)),
            device_id_type=MESH,
        )

    load_down.wait()
    own_part, adapter = {}, {}
    for group in reversed(range(GROUPS)):
        first = group * group_hosts
        arrived(tables.at[first : first + group_hosts], table_recv.at[group])
        adapter[group], adapter_lane = adapters(group)
        arrived(rows_in.at[first : first + group_hosts], rows_recv.at[group])
        x = unpack(rows_in[first : first + group_hosts])
        folded = jnp.zeros((rank, group_rows), F32)
        for c in range(0, owned_total, 4):
            s = dot(down_ref[c : c + 4].reshape(4 * rank, 2 * half), x, NT)
            for i in range(4):
                folded = folded + jnp.where(
                    adapter_lane == float(c + i), s[i * rank : (i + 1) * rank], 0.0
                )
        own_part[group] = folded
        part_out[group] = folded.astype(BF)
        for step in (4, 5, 3, 2, 6, 7, 1):
            part_copy(group, step).start()

    arrived(base_in, base_recv)
    base = out_ref[...]
    for i in range(chips - 1):
        base = base + base_in[i].astype(F32)
    out_ref[...] = base

    def back_copy(step):
        other = behind(host, step)
        return pltpu.make_async_remote_copy(
            src_ref=back_out.at[step],
            dst_ref=back_in.at[host],
            send_sem=back_send,
            recv_sem=back_recv,
            device_id=(other, lane),
            device_id_type=MESH,
        )

    load_up.wait()
    for group in reversed(range(GROUPS)):
        arrived(part_in.at[group], part_recv.at[group])
        g = own_part[group]
        for step in range(1, n_tp):
            g = g + part_in[group, step - 1].astype(F32)
        full = jnp.concatenate([g, g], axis=0).T
        raised = jnp.zeros((group_rows, 2 * half), F32)
        for c in range(0, owned_total, 4):
            e = jnp.concatenate(
                [
                    jnp.where(adapter[group] == float(c), full, 0.0),
                    jnp.where(adapter[group] == float(c + 2), full, 0.0),
                ],
                axis=1,
            ).astype(BF)
            raised = raised + dot(e, up_ref[c : c + 4].reshape(4 * rank, 2 * half))
        first = group * group_hosts
        back_out[first : first + group_hosts] = pack(raised[:, :half], raised[:, half:])
        for step in range(first, min(first + group_hosts, last)):
            back_copy(step).start()

    pltpu.make_async_copy(back_out.at[last], back_in.at[host], back_recv).start()
    arrived(back_in, back_recv)
    y = back_in[...].reshape(n_hst * 16, half)
    out_ref[:, :half] += ADAPTER_SCALE * dot(gather_lo, y)
    out_ref[:, half:] += ADAPTER_SCALE * dot(gather_hi, y)

    arrived(tables.at[0:last], table_send)
    arrived(rows_out.at[0:last], rows_send)
    arrived(back_out.at[0:last], back_send)
    arrived(base_out, base_send)
    arrived(part_in, part_send)


def local(
    queries,
    key_page_cache,
    value_page_cache,
    request_pages,
    context_length,
    output_weight,
    adapter_down_weight,
    adapter_up_weight,
    residual,
    host_slot_adapter,
    request_slot,
):
    n_hst, n_tp = lax.axis_size("hst"), lax.axis_size("tp")
    rows, width = queries.shape
    any_spec = pl.BlockSpec(memory_space=pl.ANY)
    dma = pltpu.SemaphoreType.DMA
    block = (n_hst, 16, width // 2)
    part_rows = n_hst * 8 // GROUPS // 2
    arguments = (
        queries,
        key_page_cache,
        value_page_cache,
        request_pages.T,
        context_length.reshape(1, -1),
        output_weight,
        adapter_down_weight,
        adapter_up_weight,
        host_slot_adapter.reshape(1, -1),
        request_slot.T,
    )
    summed = pl.pallas_call(
        functools.partial(kernel, n_hst, n_tp),
        out_shape=jax.ShapeDtypeStruct((rows, width), F32),
        in_specs=[any_spec] * len(arguments),
        out_specs=pl.BlockSpec(memory_space=pltpu.VMEM),
        scratch_shapes=[
            pltpu.SMEM(request_pages.shape[::-1], jnp.int32),
            pltpu.VMEM((1, rows), jnp.int32),
            pltpu.VMEM((1, host_slot_adapter.shape[0]), jnp.int32),
            pltpu.VMEM((1, rows), jnp.int32),
            pltpu.VMEM(queries.shape, BF),
            pltpu.VMEM((rows * width // HD, HD), F32),
            pltpu.VMEM(key_page_cache.shape, BF),
            pltpu.VMEM(value_page_cache.shape, BF),
            pltpu.VMEM(output_weight.shape, BF),
            pltpu.VMEM(adapter_down_weight.shape, BF),
            pltpu.VMEM(adapter_up_weight.shape, BF),
            pltpu.VMEM(queries.shape, F32),
            pltpu.VMEM((8, 128), jnp.int32),
            pltpu.VMEM((n_hst, 128), jnp.int32),
            pltpu.VMEM(block, BF),
            pltpu.VMEM(block, BF),
            pltpu.VMEM(block, BF),
            pltpu.VMEM(block, BF),
            pltpu.VMEM((n_tp // 2, rows, width), BF),
            pltpu.VMEM((n_tp // 2, rows, width), BF),
            pltpu.VMEM((n_tp // 2, rows, width), F32),
            pltpu.VMEM((n_tp // 2 - 1, rows, width), BF),
            pltpu.VMEM((n_tp // 2 - 1, rows, width), BF),
            pltpu.VMEM((GROUPS, part_rows, 128), BF),
            pltpu.VMEM((GROUPS, n_tp - 1, part_rows, 128), BF),
            dma((10,)),
            dma,
            dma((GROUPS,)),
            dma,
            dma((GROUPS,)),
            dma,
            dma,
            dma,
            dma,
            dma,
            dma,
            dma,
            dma((GROUPS,)),
        ],
        compiler_params=pltpu.CompilerParams(
            collective_id=0, has_side_effects=True, vmem_limit_bytes=40 * 1024 * 1024
        ),
        cost_estimate=pl.CostEstimate(
            flops=2_000_000_000, bytes_accessed=12_000_000, transcendentals=32768
        ),
        name="decode_step",
    )(*(pltpu.with_memory_space_constraint(a, pltpu.HBM) for a in arguments))
    return (residual.astype(F32) + summed).astype(BF)


def solution(mesh):
    in_specs = (
        P("hst", "tp"),
        P("hst", None, "tp"),
        P("hst", None, "tp"),
        P("hst", None),
        P("hst"),
        P("tp", None),
        P("hst", None, "tp"),
        P("hst", None, "tp"),
        P("hst", "tp"),
        P("hst"),
        P("hst", None),
    )
    out_specs = P("hst", "tp")
    return jax.shard_map(local, mesh=mesh, in_specs=in_specs, out_specs=out_specs, check_vma=False)
```

```python
import functools
import math

import jax
import jax.numpy as jnp
from jax import lax
from jax.experimental import pallas as pl
from jax.experimental.pallas import tpu as pltpu
from jax.sharding import PartitionSpec as P

HD = 128
ADAPTER_SCALE = 2.0
Z, X = 8, 4
GROUPS = 4
MESH = pl.DeviceIdType.MESH
BF = jnp.bfloat16
F32 = jnp.float32
NT = (((1,), (1,)), ((), ()))
NN = (((1,), (0,)), ((), ()))


def dot(a, b, dims=NN):
    return lax.dot_general(a, b, dims, preferred_element_type=F32)


def iota(shape, dim):
    return lax.broadcasted_iota(jnp.int32, shape, dim)


def offsets(step):
    i, j = step // Z, step % Z
    dz = Z // 2 + (1 - 2 * (j % 2)) * ((j + 1) // 2)
    return dz, (2, 3, 1, 0)[i]


def ahead_of(host, step):
    dz, dx = offsets(step)
    return lax.rem(host // X + dz, Z) * X + lax.rem(lax.rem(host, X) + dx, X)


def behind(host, step):
    dz, dx = offsets(step)
    return lax.rem(host // X + Z - dz, Z) * X + lax.rem(lax.rem(host, X) + X - dx, X)


def kernel(
    n_hst,
    n_tp,
    q_hbm,
    k_hbm,
    v_hbm,
    pages_hbm,
    length_hbm,
    w_hbm,
    down_hbm,
    up_hbm,
    table_hbm,
    slot_hbm,
    out_ref,
    pages_ref,
    length_ref,
    table_ref,
    slot_ref,
    q_ref,
    logits_ref,
    k_ref,
    v_ref,
    w_ref,
    down_ref,
    up_ref,
    att_ref,
    table_out,
    tables,
    rows_out,
    rows_in,
    back_out,
    back_in,
    pair_out,
    pair_in,
    base_own,
    base_out,
    base_in,
    part_out,
    part_in,
    local_sem,
    table_send,
    table_recv,
    rows_send,
    rows_recv,
    back_send,
    back_recv,
    pair_send,
    pair_recv,
    base_send,
    base_recv,
    part_send,
    part_recv,
):
    host = lax.axis_index("hst")
    lane = lax.axis_index("tp")

    def load(src, dst, i):
        return pltpu.make_async_copy(src, dst, local_sem.at[i])

    load_table = load(table_hbm, table_ref, 0)
    load_slot = load(slot_hbm, slot_ref, 1)
    load_pages = load(pages_hbm, pages_ref, 2)
    load_length = load(length_hbm, length_ref, 3)
    load_q = load(q_hbm, q_ref, 4)
    load_k = load(k_hbm, k_ref, 5)
    load_v = load(v_hbm, v_ref, 6)
    load_w = load(w_hbm, w_ref, 7)
    load_down = load(down_hbm, down_ref, 8)
    load_up = load(up_hbm, up_ref, 9)
    load_pages.start()
    load_q.start()
    load_k.start()
    load_length.start()
    load_table.start()
    load_slot.start()
    load_v.start()

    barrier = pltpu.get_barrier_semaphore()

    def greet_hosts(step):
        other = ahead_of(host, step)
        pl.semaphore_signal(barrier, inc=1, device_id=(other, lane), device_id_type=MESH)

    def greet_lanes(step):
        other = lax.rem(lane + step, n_tp)
        pl.semaphore_signal(barrier, inc=1, device_id=(host, other), device_id_type=MESH)

    for step in range(n_hst - 1):
        greet_hosts(step)
    for step in range(1, n_tp):
        greet_lanes(step)

    slots = table_ref.shape[1]
    row_total = slot_ref.shape[1]
    load_table.wait()
    load_slot.wait()
    table_out[...] = jnp.full(table_out.shape, -1, jnp.int32)
    table_out[0:1, 0:slots] = table_ref[...]
    table_row = table_out[0:1, :]
    owner_row = jnp.right_shift(table_row, 5)
    owner_all = jnp.broadcast_to(owner_row, (128, 128))
    s_sub, s_lane = iota((128, 128), 0), iota((128, 128), 1)
    owner_col = jnp.sum(jnp.where(s_sub == s_lane, owner_all, 0), axis=1, keepdims=True)
    place_row = jnp.sum(
        jnp.where((owner_col == owner_all) & (s_sub < s_lane), 1, 0), axis=0, keepdims=True
    )
    dz = jnp.bitwise_and(jnp.right_shift(owner_row, 2) - host // X + Z, Z - 1)
    dx = jnp.bitwise_and(jnp.bitwise_and(owner_row, X - 1) - lax.rem(host, X) + X, X - 1)
    z_order = jnp.where(dz >= Z // 2, 2 * dz - Z, Z - 1 - 2 * dz)
    x_order = jnp.where(dx >= X // 2, dx - X // 2, X - 1 - dx)
    start_row = (x_order * Z + z_order) * 8 + place_row * 4
    chosen_row = slot_ref[...]
    r_sub, r_lane = iota((row_total, 128), 0), iota((row_total, 128), 1)
    q_sub, q_lane = iota((row_total, row_total), 0), iota((row_total, row_total), 1)
    chosen_col = jnp.sum(jnp.where(q_sub == q_lane, chosen_row, 0), axis=1, keepdims=True)
    before_col = jnp.sum(
        jnp.where((chosen_col == chosen_row) & (q_lane < q_sub), 1, 0), axis=1, keepdims=True
    )
    target_col = before_col + jnp.sum(
        jnp.where(chosen_col == r_lane, start_row, 0), axis=1, keepdims=True
    )
    target_row = jnp.sum(jnp.where(r_sub == r_lane, target_col, 0), axis=0, keepdims=True)
    send_total = n_hst * 8
    scatter = jnp.where(
        iota((send_total, row_total), 0) == target_row[:, :row_total], 1.0, 0.0
    ).astype(BF)
    back_place = (target_col // 8) * 16 + lax.rem(target_col, 8)
    back_lane = iota((row_total, n_hst * 16), 1)
    gather_lo = jnp.where(back_lane == back_place, 1.0, 0.0).astype(BF)
    gather_hi = jnp.where(back_lane == back_place + 8, 1.0, 0.0).astype(BF)

    heads = q_ref.shape[1] // HD
    tall = heads * 8
    load_length.wait()
    row = iota((row_total * heads, row_total), 0)
    request = row // tall * 8 + lax.rem(row, 8)
    length_col = jnp.sum(
        jnp.where(iota(row.shape, 1) == request, length_ref[...], 0), axis=1, keepdims=True
    )

    load_pages.wait()
    load_q.wait()
    load_k.wait()
    load_w.start()
    load_down.start()
    load_up.start()
    sub = iota((8, HD), 0)

    def pages_of(ref, row):
        return [ref[pages_ref[p, row]] for p in range(pages_ref.shape[0])]

    def pair_of(ref, row):
        return jnp.concatenate(pages_of(ref, row) + pages_of(ref, row + 1), axis=0)

    def match(step, carry):
        first = pl.multiple_of(step * 16, 16)
        q16 = q_ref[pl.ds(first, 16), :].astype(F32)
        for part in range(2):
            q = q16[part * 8 : (part + 1) * 8]
            q = jnp.concatenate([q[:, j * HD : (j + 1) * HD] for j in range(heads)], axis=0).astype(BF)
            got = [jnp.zeros((8, HD), F32)] * heads
            for r in range(0, 8, 2):
                s = dot(q, pair_of(k_ref, first + part * 8 + r), NT)
                for j in range(heads):
                    rows8 = s[j * 8 : (j + 1) * 8]
                    got[j] = jnp.where(sub == r, rows8[:, :HD], got[j])
                    got[j] = jnp.where(sub == r + 1, rows8[:, HD:], got[j])
            logits_ref[pl.ds(pl.multiple_of((step * 2 + part) * tall, tall), tall), :] = jnp.concatenate(
                got, axis=0
            )
        return carry

    lax.fori_loop(0, row_total // 16, match, 0)

    live = iota((row_total * heads, HD), 1) < length_col
    logits = jnp.where(live, logits_ref[...] * (1.0 / math.sqrt(HD)), -jnp.inf)
    e = jnp.exp(logits - jnp.max(logits, axis=1, keepdims=True))
    logits_ref[...] = e / jnp.sum(e, axis=1, keepdims=True)

    load_v.wait()

    def blend(step, carry):
        first = pl.multiple_of(step * 16, 16)
        for part in range(2):
            p = logits_ref[pl.ds(pl.multiple_of((step * 2 + part) * tall, tall), tall), :]
            p = [p[j * 8 : (j + 1) * 8] for j in range(heads)]
            acc = jnp.zeros((tall, HD), F32)
            for r in range(0, 8, 2):
                spread = jnp.concatenate(
                    [
                        jnp.concatenate([jnp.where(sub == r + i, x, 0.0) for x in p], axis=0)
                        for i in range(2)
                    ],
                    axis=1,
                )
                acc = acc + dot(spread.astype(BF), pair_of(v_ref, first + part * 8 + r))
            for j in range(heads):
                att_ref[pl.ds(first + part * 8, 8), j * HD : (j + 1) * HD] = acc[j * 8 : (j + 1) * 8]
        return carry

    lax.fori_loop(0, row_total // 16, blend, 0)

    att = att_ref[...].astype(BF)
    half = att.shape[1] // 2

    def pack(lo, hi):
        blocks = lo.shape[0] // 8
        return jnp.concatenate(
            [lo.reshape(blocks, 8, half), hi.reshape(blocks, 8, half)], axis=1
        ).astype(BF)

    def unpack(x):
        rows = x.shape[0] * 8
        x = x.astype(F32)
        lo, hi = x[:, :8].reshape(rows, half), x[:, 8:].reshape(rows, half)
        return jnp.concatenate([lo, hi], axis=1).astype(BF)


    def arrived(ref, sem):
        pltpu.make_async_copy(ref, ref, sem).wait()

    def table_copy(step, group):
        return pltpu.make_async_remote_copy(
            src_ref=table_out.at[0:1, :],
            dst_ref=tables.at[pl.ds(step, 1), :],
            send_sem=table_send,
            recv_sem=table_recv.at[group],
            device_id=(ahead_of(host, step), lane),
            device_id_type=MESH,
        )

    def rows_copy(step, group):
        return pltpu.make_async_remote_copy(
            src_ref=rows_out.at[step],
            dst_ref=rows_in.at[step],
            send_sem=rows_send,
            recv_sem=rows_recv.at[group],
            device_id=(ahead_of(host, step), lane),
            device_id_type=MESH,
        )

    group_hosts = n_hst // GROUPS
    last = n_hst - 1

    pl.semaphore_wait(barrier, n_hst - 1 + n_tp - 1)
    for group in range(GROUPS):
        first = group * group_hosts
        spread = dot(scatter[first * 8 : (first + group_hosts) * 8], att)
        rows_out[first : first + group_hosts] = pack(spread[:, :half], spread[:, half:])
        for step in range(first, min(first + group_hosts, last)):
            table_copy(step, group).start()
            rows_copy(step, group).start()
    pltpu.make_async_copy(
        table_out.at[0:1, :], tables.at[last : last + 1, :], table_recv.at[GROUPS - 1]
    ).start()
    pltpu.make_async_copy(rows_out.at[last], rows_in.at[last], rows_recv.at[GROUPS - 1]).start()

    load_w.wait()
    width = out_ref.shape[1]
    chips = n_tp // 2
    chip, core = lane // 2, lax.rem(lane, 2)
    turns = (2, 1, 3, 0)

    def project(which):
        return dot(att, w_ref[:, pl.ds(pl.multiple_of(which * width, width), width)])

    def chip_at(turn):
        return lax.rem(chip + turn, chips)

    def pair_copy():
        return pltpu.make_async_remote_copy(
            src_ref=pair_out,
            dst_ref=pair_in,
            send_sem=pair_send,
            recv_sem=pair_recv,
            device_id=(host, lane + 1 - 2 * core),
            device_id_type=MESH,
        )

    def base_copy(i):
        return pltpu.make_async_remote_copy(
            src_ref=base_out.at[i],
            dst_ref=base_in.at[i],
            send_sem=base_send,
            recv_sem=base_recv,
            device_id=(host, 2 * chip_at(turns[i]) + core),
            device_id_type=MESH,
        )

    for i, turn in enumerate(turns):
        pair_out[i] = project(2 * chip_at(turn) + 1 - core).astype(BF)
    pair_copy().start()
    for i, turn in enumerate(turns):
        base_own[i] = project(2 * chip_at(turn) + core)
    pair_copy().wait()
    for i in range(chips - 1):
        base_out[i] = (base_own[i] + pair_in[i].astype(F32)).astype(BF)
        base_copy(i).start()
    out_ref[...] = base_own[chips - 1] + pair_in[chips - 1].astype(F32)

    group_rows = group_hosts * 8
    owned_total, rank, _ = down_ref.shape
    place_sub, place_lane = iota((group_rows, 128), 0), iota((group_rows, 128), 1)
    from_host = iota((group_rows, group_hosts), 0) // 8 == iota((group_rows, group_hosts), 1)
    from_host = jnp.where(from_host, 1.0, 0.0).astype(BF)
    earlier = jnp.where(s_sub < s_lane, 1.0, 0.0).astype(BF)

    def adapters(group):
        first = group * group_hosts
        table = tables[first : first + group_hosts]
        owned = jnp.right_shift(table, 5) == host
        ahead = dot(jnp.where(owned, 1.0, 0.0).astype(BF), earlier)
        local_index = jnp.bitwise_and(table, 31).astype(F32)

        def place_index(place):
            got = jnp.where(owned & (ahead == place), local_index, -1.0)
            got = jnp.broadcast_to(jnp.max(got, axis=1, keepdims=True), got.shape).astype(BF)
            return dot(from_host, got)

        found = jnp.where(lax.rem(place_sub, 8) < 4, place_index(0.0), place_index(1.0))
        return found - jnp.where(place_lane >= 64, 1.0, 0.0), found.T[:rank]


    def part_copy(group, step):
        return pltpu.make_async_remote_copy(
            src_ref=part_out.at[group],
            dst_ref=part_in.at[group, step - 1],
            send_sem=part_send,
            recv_sem=part_recv.at[group],
            device_id=(host, lax.rem(lane + step, n_tp)),
            device_id_type=MESH,
        )

    load_down.wait()
    own_part, adapter = {}, {}
    for group in range(GROUPS):
        first = group * group_hosts
        arrived(tables.at[first : first + group_hosts], table_recv.at[group])
        adapter[group], adapter_lane = adapters(group)
        arrived(rows_in.at[first : first + group_hosts], rows_recv.at[group])
        x = unpack(rows_in[first : first + group_hosts])
        folded = jnp.zeros((rank, group_rows), F32)
        for c in range(0, owned_total, 4):
            s = dot(down_ref[c : c + 4].reshape(4 * rank, 2 * half), x, NT)
            for i in range(4):
                folded = folded + jnp.where(
                    adapter_lane == float(c + i), s[i * rank : (i + 1) * rank], 0.0
                )
        own_part[group] = folded
        part_out[group] = jnp.concatenate([folded[: rank // 2], folded[rank // 2 :]], axis=1).astype(BF)
        for step in (4, 5, 3, 2, 6, 7, 1):
            part_copy(group, step).start()

    arrived(base_in, base_recv)
    base = out_ref[...]
    for i in range(chips - 1):
        base = base + base_in[i].astype(F32)
    out_ref[...] = base

    def back_copy(step, group):
        other = behind(host, step)
        return pltpu.make_async_remote_copy(
            src_ref=back_out.at[step],
            dst_ref=back_in.at[step],
            send_sem=back_send,
            recv_sem=back_recv.at[group],
            device_id=(other, lane),
            device_id_type=MESH,
        )

    load_up.wait()
    for group in range(GROUPS):
        arrived(part_in.at[group], part_recv.at[group])
        g = part_in[group, 0].astype(F32)
        for step in range(2, n_tp):
            g = g + part_in[group, step - 1].astype(F32)
        g = own_part[group] + jnp.concatenate([g[:, :group_rows], g[:, group_rows:]], axis=0)
        full = jnp.concatenate([g, g], axis=0).T
        raised = jnp.zeros((group_rows, 2 * half), F32)
        for c in range(0, owned_total, 4):
            e = jnp.concatenate(
                [
                    jnp.where(adapter[group] == float(c), full, 0.0),
                    jnp.where(adapter[group] == float(c + 2), full, 0.0),
                ],
                axis=1,
            ).astype(BF)
            raised = raised + dot(e, up_ref[c : c + 4].reshape(4 * rank, 2 * half))
        first = group * group_hosts
        back_out[first : first + group_hosts] = pack(raised[:, :half], raised[:, half:])
        for step in range(first, min(first + group_hosts, last)):
            back_copy(step, group).start()

    pltpu.make_async_copy(back_out.at[last], back_in.at[last], back_recv.at[GROUPS - 1]).start()
    given_lo, given_hi = 0.0, 0.0
    for group in range(GROUPS):
        first = group * group_hosts
        arrived(back_in.at[first : first + group_hosts], back_recv.at[group])
        y = back_in[first : first + group_hosts].reshape(group_hosts * 16, half)
        mine = slice(first * 16, (first + group_hosts) * 16)
        given_lo = given_lo + dot(gather_lo[:, mine], y)
        given_hi = given_hi + dot(gather_hi[:, mine], y)
    out_ref[:, :half] += ADAPTER_SCALE * given_lo
    out_ref[:, half:] += ADAPTER_SCALE * given_hi

    arrived(tables.at[0:last], table_send)
    arrived(rows_out.at[0:last], rows_send)
    arrived(back_out.at[0:last], back_send)
    arrived(base_out, base_send)
    arrived(part_in, part_send)


def local(
    queries,
    key_page_cache,
    value_page_cache,
    request_pages,
    context_length,
    output_weight,
    adapter_down_weight,
    adapter_up_weight,
    residual,
    host_slot_adapter,
    request_slot,
):
    n_hst, n_tp = lax.axis_size("hst"), lax.axis_size("tp")
    rows, width = queries.shape
    any_spec = pl.BlockSpec(memory_space=pl.ANY)
    dma = pltpu.SemaphoreType.DMA
    block = (n_hst, 16, width // 2)
    part_rows = n_hst * 8 // GROUPS // 2
    arguments = (
        queries,
        key_page_cache,
        value_page_cache,
        request_pages.T,
        context_length.reshape(1, -1),
        output_weight,
        adapter_down_weight,
        adapter_up_weight,
        host_slot_adapter.reshape(1, -1),
        request_slot.T,
    )
    summed = pl.pallas_call(
        functools.partial(kernel, n_hst, n_tp),
        out_shape=jax.ShapeDtypeStruct((rows, width), F32),
        in_specs=[any_spec] * len(arguments),
        out_specs=pl.BlockSpec(memory_space=pltpu.VMEM),
        scratch_shapes=[
            pltpu.SMEM(request_pages.shape[::-1], jnp.int32),
            pltpu.VMEM((1, rows), jnp.int32),
            pltpu.VMEM((1, host_slot_adapter.shape[0]), jnp.int32),
            pltpu.VMEM((1, rows), jnp.int32),
            pltpu.VMEM(queries.shape, BF),
            pltpu.VMEM((rows * width // HD, HD), F32),
            pltpu.VMEM(key_page_cache.shape, BF),
            pltpu.VMEM(value_page_cache.shape, BF),
            pltpu.VMEM(output_weight.shape, BF),
            pltpu.VMEM(adapter_down_weight.shape, BF),
            pltpu.VMEM(adapter_up_weight.shape, BF),
            pltpu.VMEM(queries.shape, F32),
            pltpu.VMEM((8, 128), jnp.int32),
            pltpu.VMEM((n_hst, 128), jnp.int32),
            pltpu.VMEM(block, BF),
            pltpu.VMEM(block, BF),
            pltpu.VMEM(block, BF),
            pltpu.VMEM(block, BF),
            pltpu.VMEM((n_tp // 2, rows, width), BF),
            pltpu.VMEM((n_tp // 2, rows, width), BF),
            pltpu.VMEM((n_tp // 2, rows, width), F32),
            pltpu.VMEM((n_tp // 2 - 1, rows, width), BF),
            pltpu.VMEM((n_tp // 2 - 1, rows, width), BF),
            pltpu.VMEM((GROUPS, part_rows, 128), BF),
            pltpu.VMEM((GROUPS, n_tp - 1, part_rows, 128), BF),
            dma((10,)),
            dma,
            dma((GROUPS,)),
            dma,
            dma((GROUPS,)),
            dma,
            dma((GROUPS,)),
            dma,
            dma,
            dma,
            dma,
            dma,
            dma((GROUPS,)),
        ],
        compiler_params=pltpu.CompilerParams(
            collective_id=0, has_side_effects=True, vmem_limit_bytes=40 * 1024 * 1024
        ),
        cost_estimate=pl.CostEstimate(
            flops=2_000_000_000, bytes_accessed=12_000_000, transcendentals=32768
        ),
        name="decode_step",
    )(*(pltpu.with_memory_space_constraint(a, pltpu.HBM) for a in arguments))
    return (residual.astype(F32) + summed).astype(BF)


def solution(mesh):
    in_specs = (
        P("hst", "tp"),
        P("hst", None, "tp"),
        P("hst", None, "tp"),
        P("hst", None),
        P("hst"),
        P("tp", None),
        P("hst", None, "tp"),
        P("hst", None, "tp"),
        P("hst", "tp"),
        P("hst"),
        P("hst", None),
    )
    out_specs = P("hst", "tp")
    return jax.shard_map(local, mesh=mesh, in_specs=in_specs, out_specs=out_specs, check_vma=False)
```

```python
import functools
import math

import jax
import jax.numpy as jnp
from jax import lax
from jax.experimental import pallas as pl
from jax.experimental.pallas import tpu as pltpu
from jax.sharding import PartitionSpec as P

HD = 128
ADAPTER_SCALE = 2.0
Z, X = 8, 4
GROUPS = 4
MESH = pl.DeviceIdType.MESH
BF = jnp.bfloat16
F32 = jnp.float32
NT = (((1,), (1,)), ((), ()))
NN = (((1,), (0,)), ((), ()))


def dot(a, b, dims=NN):
    return lax.dot_general(a, b, dims, preferred_element_type=F32)


def iota(shape, dim):
    return lax.broadcasted_iota(jnp.int32, shape, dim)


def offsets(step):
    i, j = step // Z, step % Z
    dz = Z // 2 + (1 - 2 * (j % 2)) * ((j + 1) // 2)
    return dz, (2, 3, 1, 0)[i]


def ahead_of(host, step):
    dz, dx = offsets(step)
    return lax.rem(host // X + dz, Z) * X + lax.rem(lax.rem(host, X) + dx, X)


def behind(host, step):
    dz, dx = offsets(step)
    return lax.rem(host // X + Z - dz, Z) * X + lax.rem(lax.rem(host, X) + X - dx, X)


def kernel(
    n_hst,
    n_tp,
    q_hbm,
    k_hbm,
    v_hbm,
    pages_hbm,
    length_hbm,
    w_hbm,
    down_hbm,
    up_hbm,
    table_hbm,
    slot_hbm,
    out_ref,
    pages_ref,
    length_ref,
    table_ref,
    slot_ref,
    q_ref,
    logits_ref,
    k_ref,
    v_ref,
    w_ref,
    down_ref,
    up_ref,
    att_ref,
    table_out,
    tables,
    rows_out,
    rows_in,
    back_out,
    back_in,
    pair_out,
    pair_in,
    base_own,
    base_out,
    base_in,
    part_out,
    part_in,
    local_sem,
    table_send,
    table_recv,
    rows_send,
    rows_recv,
    back_send,
    back_recv,
    pair_send,
    pair_recv,
    base_send,
    base_recv,
    part_send,
    part_recv,
):
    host = lax.axis_index("hst")
    lane = lax.axis_index("tp")

    def load(src, dst, i):
        return pltpu.make_async_copy(src, dst, local_sem.at[i])

    load_table = load(table_hbm, table_ref, 0)
    load_slot = load(slot_hbm, slot_ref, 1)
    load_pages = load(pages_hbm, pages_ref, 2)
    load_length = load(length_hbm, length_ref, 3)
    load_q = load(q_hbm, q_ref, 4)
    load_k = load(k_hbm, k_ref, 5)
    load_v = load(v_hbm, v_ref, 6)
    load_w = load(w_hbm, w_ref, 7)
    load_down = load(down_hbm, down_ref, 8)
    load_up = load(up_hbm, up_ref, 9)
    load_pages.start()
    load_q.start()
    load_k.start()
    load_length.start()
    load_table.start()
    load_slot.start()
    load_v.start()

    barrier = pltpu.get_barrier_semaphore()

    def greet_hosts(step):
        other = ahead_of(host, step)
        pl.semaphore_signal(barrier, inc=1, device_id=(other, lane), device_id_type=MESH)

    def greet_lanes(step):
        other = lax.rem(lane + step, n_tp)
        pl.semaphore_signal(barrier, inc=1, device_id=(host, other), device_id_type=MESH)

    for step in range(n_hst - 1):
        greet_hosts(step)
    for step in range(1, n_tp):
        greet_lanes(step)

    slots = table_ref.shape[1]
    row_total = slot_ref.shape[1]
    load_table.wait()
    load_slot.wait()
    table_out[...] = jnp.full(table_out.shape, -1, jnp.int32)
    table_out[0:1, 0:slots] = table_ref[...]
    table_row = table_out[0:1, :]
    owner_row = jnp.right_shift(table_row, 5)
    owner_all = jnp.broadcast_to(owner_row, (128, 128))
    s_sub, s_lane = iota((128, 128), 0), iota((128, 128), 1)
    owner_col = jnp.sum(jnp.where(s_sub == s_lane, owner_all, 0), axis=1, keepdims=True)
    place_row = jnp.sum(
        jnp.where((owner_col == owner_all) & (s_sub < s_lane), 1, 0), axis=0, keepdims=True
    )
    dz = jnp.bitwise_and(jnp.right_shift(owner_row, 2) - host // X + Z, Z - 1)
    dx = jnp.bitwise_and(jnp.bitwise_and(owner_row, X - 1) - lax.rem(host, X) + X, X - 1)
    z_order = jnp.where(dz >= Z // 2, 2 * dz - Z, Z - 1 - 2 * dz)
    x_order = jnp.where(dx >= X // 2, dx - X // 2, X - 1 - dx)
    start_row = (x_order * Z + z_order) * 8 + place_row * 4
    chosen_row = slot_ref[...]
    r_sub, r_lane = iota((row_total, 128), 0), iota((row_total, 128), 1)
    q_sub, q_lane = iota((row_total, row_total), 0), iota((row_total, row_total), 1)
    chosen_col = jnp.sum(jnp.where(q_sub == q_lane, chosen_row, 0), axis=1, keepdims=True)
    before_col = jnp.sum(
        jnp.where((chosen_col == chosen_row) & (q_lane < q_sub), 1, 0), axis=1, keepdims=True
    )
    target_col = before_col + jnp.sum(
        jnp.where(chosen_col == r_lane, start_row, 0), axis=1, keepdims=True
    )
    target_row = jnp.sum(jnp.where(r_sub == r_lane, target_col, 0), axis=0, keepdims=True)
    send_total = n_hst * 8
    scatter = jnp.where(
        iota((send_total, row_total), 0) == target_row[:, :row_total], 1.0, 0.0
    ).astype(BF)
    back_place = (target_col // 8) * 16 + lax.rem(target_col, 8)
    back_lane = iota((row_total, n_hst * 16), 1)
    gather_lo = jnp.where(back_lane == back_place, 1.0, 0.0).astype(BF)
    gather_hi = jnp.where(back_lane == back_place + 8, 1.0, 0.0).astype(BF)

    heads = q_ref.shape[1] // HD
    tall = heads * 8
    load_length.wait()
    row = iota((row_total * heads, row_total), 0)
    request = row // tall * 8 + lax.rem(row, 8)
    length_col = jnp.sum(
        jnp.where(iota(row.shape, 1) == request, length_ref[...], 0), axis=1, keepdims=True
    )

    load_pages.wait()
    load_q.wait()
    load_k.wait()
    load_w.start()
    load_down.start()
    load_up.start()
    sub = iota((8, HD), 0)

    def pages_of(ref, row):
        return [ref[pages_ref[p, row]] for p in range(pages_ref.shape[0])]

    def pair_of(ref, row):
        return jnp.concatenate(pages_of(ref, row) + pages_of(ref, row + 1), axis=0)

    def match(step, carry):
        first = pl.multiple_of(step * 16, 16)
        q16 = q_ref[pl.ds(first, 16), :].astype(F32)
        for part in range(2):
            q = q16[part * 8 : (part + 1) * 8]
            q = jnp.concatenate([q[:, j * HD : (j + 1) * HD] for j in range(heads)], axis=0).astype(BF)
            got = [jnp.zeros((8, HD), F32)] * heads
            for r in range(0, 8, 2):
                s = dot(q, pair_of(k_ref, first + part * 8 + r), NT)
                for j in range(heads):
                    rows8 = s[j * 8 : (j + 1) * 8]
                    got[j] = jnp.where(sub == r, rows8[:, :HD], got[j])
                    got[j] = jnp.where(sub == r + 1, rows8[:, HD:], got[j])
            logits_ref[pl.ds(pl.multiple_of((step * 2 + part) * tall, tall), tall), :] = jnp.concatenate(
                got, axis=0
            )
        return carry

    lax.fori_loop(0, row_total // 16, match, 0)

    live = iota((row_total * heads, HD), 1) < length_col
    logits = jnp.where(live, logits_ref[...] * (1.0 / math.sqrt(HD)), -jnp.inf)
    e = jnp.exp(logits - jnp.max(logits, axis=1, keepdims=True))
    logits_ref[...] = e / jnp.sum(e, axis=1, keepdims=True)

    load_v.wait()

    def blend(step, carry):
        first = pl.multiple_of(step * 16, 16)
        for part in range(2):
            p = logits_ref[pl.ds(pl.multiple_of((step * 2 + part) * tall, tall), tall), :]
            p = [p[j * 8 : (j + 1) * 8] for j in range(heads)]
            acc = jnp.zeros((tall, HD), F32)
            for r in range(0, 8, 2):
                spread = jnp.concatenate(
                    [
                        jnp.concatenate([jnp.where(sub == r + i, x, 0.0) for x in p], axis=0)
                        for i in range(2)
                    ],
                    axis=1,
                )
                acc = acc + dot(spread.astype(BF), pair_of(v_ref, first + part * 8 + r))
            for j in range(heads):
                att_ref[pl.ds(first + part * 8, 8), j * HD : (j + 1) * HD] = acc[j * 8 : (j + 1) * 8]
        return carry

    lax.fori_loop(0, row_total // 16, blend, 0)

    att = att_ref[...].astype(BF)
    half = att.shape[1] // 2

    def pack(lo, hi):
        blocks = lo.shape[0] // 8
        return jnp.concatenate(
            [lo.reshape(blocks, 8, half), hi.reshape(blocks, 8, half)], axis=1
        ).astype(BF)

    def unpack(x):
        rows = x.shape[0] * 8
        x = x.astype(F32)
        lo, hi = x[:, :8].reshape(rows, half), x[:, 8:].reshape(rows, half)
        return jnp.concatenate([lo, hi], axis=1).astype(BF)


    def arrived(ref, sem):
        pltpu.make_async_copy(ref, ref, sem).wait()

    def table_copy(step, group):
        return pltpu.make_async_remote_copy(
            src_ref=table_out.at[0:1, :],
            dst_ref=tables.at[pl.ds(step, 1), :],
            send_sem=table_send,
            recv_sem=table_recv.at[group],
            device_id=(ahead_of(host, step), lane),
            device_id_type=MESH,
        )

    def rows_copy(step, group):
        return pltpu.make_async_remote_copy(
            src_ref=rows_out.at[step],
            dst_ref=rows_in.at[step],
            send_sem=rows_send,
            recv_sem=rows_recv.at[group],
            device_id=(ahead_of(host, step), lane),
            device_id_type=MESH,
        )

    group_hosts = n_hst // GROUPS
    last = n_hst - 1

    pl.semaphore_wait(barrier, n_hst - 1 + n_tp - 1)
    for group in range(GROUPS):
        first = group * group_hosts
        spread = dot(scatter[first * 8 : (first + group_hosts) * 8], att)
        rows_out[first : first + group_hosts] = pack(spread[:, :half], spread[:, half:])
        for step in range(first, min(first + group_hosts, last)):
            table_copy(step, group).start()
            rows_copy(step, group).start()
    pltpu.make_async_copy(
        table_out.at[0:1, :], tables.at[last : last + 1, :], table_recv.at[GROUPS - 1]
    ).start()
    pltpu.make_async_copy(rows_out.at[last], rows_in.at[last], rows_recv.at[GROUPS - 1]).start()

    load_w.wait()
    width = out_ref.shape[1]
    chips = n_tp // 2
    chip, core = lane // 2, lax.rem(lane, 2)
    turns = (2, 1, 3, 0)

    def project(which):
        return dot(att, w_ref[:, pl.ds(pl.multiple_of(which * width, width), width)])

    def chip_at(turn):
        return lax.rem(chip + turn, chips)

    def pair_copy():
        return pltpu.make_async_remote_copy(
            src_ref=pair_out,
            dst_ref=pair_in,
            send_sem=pair_send,
            recv_sem=pair_recv,
            device_id=(host, lane + 1 - 2 * core),
            device_id_type=MESH,
        )

    def base_copy(i):
        return pltpu.make_async_remote_copy(
            src_ref=base_out.at[i],
            dst_ref=base_in.at[i],
            send_sem=base_send,
            recv_sem=base_recv,
            device_id=(host, 2 * chip_at(turns[i]) + core),
            device_id_type=MESH,
        )

    for i, turn in enumerate(turns):
        pair_out[i] = project(2 * chip_at(turn) + 1 - core).astype(BF)
    pair_copy().start()
    for i, turn in enumerate(turns):
        base_own[i] = project(2 * chip_at(turn) + core)
    pair_copy().wait()
    for i in range(chips - 1):
        base_out[i] = (base_own[i] + pair_in[i].astype(F32)).astype(BF)
        base_copy(i).start()
    out_ref[...] = base_own[chips - 1] + pair_in[chips - 1].astype(F32)

    group_rows = group_hosts * 8
    owned_total, rank, _ = down_ref.shape
    place_sub, place_lane = iota((group_rows, 128), 0), iota((group_rows, 128), 1)
    from_host = iota((group_rows, group_hosts), 0) // 8 == iota((group_rows, group_hosts), 1)
    from_host = jnp.where(from_host, 1.0, 0.0).astype(BF)
    earlier = jnp.where(s_sub < s_lane, 1.0, 0.0).astype(BF)

    def adapters(group):
        first = group * group_hosts
        table = tables[first : first + group_hosts]
        owned = jnp.right_shift(table, 5) == host
        ahead = dot(jnp.where(owned, 1.0, 0.0).astype(BF), earlier)
        local_index = jnp.bitwise_and(table, 31).astype(F32)

        def place_index(place):
            got = jnp.where(owned & (ahead == place), local_index, -1.0)
            got = jnp.broadcast_to(jnp.max(got, axis=1, keepdims=True), got.shape).astype(BF)
            return dot(from_host, got)

        found = jnp.where(lax.rem(place_sub, 8) < 4, place_index(0.0), place_index(1.0))
        return found - jnp.where(place_lane >= 64, 1.0, 0.0), found.T[:rank]


    def part_copy(group, step):
        return pltpu.make_async_remote_copy(
            src_ref=part_out.at[group],
            dst_ref=part_in.at[group, step - 1],
            send_sem=part_send,
            recv_sem=part_recv.at[group],
            device_id=(host, lax.rem(lane + step, n_tp)),
            device_id_type=MESH,
        )

    load_down.wait()
    own_part, adapter = {}, {}
    for group in range(GROUPS):
        first = group * group_hosts
        arrived(tables.at[first : first + group_hosts], table_recv.at[group])
        adapter[group], adapter_lane = adapters(group)
        arrived(rows_in.at[first : first + group_hosts], rows_recv.at[group])
        x = unpack(rows_in[first : first + group_hosts])
        folded = jnp.zeros((rank, group_rows), F32)
        for c in range(0, owned_total, 4):
            s = dot(down_ref[c : c + 4].reshape(4 * rank, 2 * half), x, NT)
            for i in range(4):
                folded = folded + jnp.where(
                    adapter_lane == float(c + i), s[i * rank : (i + 1) * rank], 0.0
                )
        own_part[group] = folded
        part_out[group] = jnp.concatenate([folded[: rank // 2], folded[rank // 2 :]], axis=1).astype(BF)
        for step in (4, 5, 3, 2, 6, 7, 1):
            part_copy(group, step).start()

    arrived(base_in, base_recv)
    base = out_ref[...]
    for i in range(chips - 1):
        base = base + base_in[i].astype(F32)
    out_ref[...] = base

    def back_copy(step, group):
        other = behind(host, step)
        return pltpu.make_async_remote_copy(
            src_ref=back_out.at[step],
            dst_ref=back_in.at[step],
            send_sem=back_send,
            recv_sem=back_recv.at[group],
            device_id=(other, lane),
            device_id_type=MESH,
        )

    load_up.wait()
    for group in range(GROUPS):
        arrived(part_in.at[group], part_recv.at[group])
        g = part_in[group, 0].astype(F32)
        for step in range(2, n_tp):
            g = g + part_in[group, step - 1].astype(F32)
        g = own_part[group] + jnp.concatenate([g[:, :group_rows], g[:, group_rows:]], axis=0)
        full = jnp.concatenate([g, g], axis=0).T
        spread_up = jnp.concatenate(
            [jnp.where(adapter[group] == float(c), full, 0.0) for c in range(0, owned_total, 2)], axis=1
        )
        raised = dot(spread_up.astype(BF), up_ref[...].reshape(owned_total * rank, 2 * half))
        first = group * group_hosts
        back_out[first : first + group_hosts] = pack(raised[:, :half], raised[:, half:])
        for step in range(first, min(first + group_hosts, last)):
            back_copy(step, group).start()

    pltpu.make_async_copy(back_out.at[last], back_in.at[last], back_recv.at[GROUPS - 1]).start()
    given_lo, given_hi = 0.0, 0.0
    for group in range(GROUPS):
        first = group * group_hosts
        arrived(back_in.at[first : first + group_hosts], back_recv.at[group])
        y = back_in[first : first + group_hosts].reshape(group_hosts * 16, half)
        mine = slice(first * 16, (first + group_hosts) * 16)
        given_lo = given_lo + dot(gather_lo[:, mine], y)
        given_hi = given_hi + dot(gather_hi[:, mine], y)
    out_ref[:, :half] += ADAPTER_SCALE * given_lo
    out_ref[:, half:] += ADAPTER_SCALE * given_hi

    arrived(tables.at[0:last], table_send)
    arrived(rows_out.at[0:last], rows_send)
    arrived(back_out.at[0:last], back_send)
    arrived(base_out, base_send)
    arrived(part_in, part_send)


def local(
    queries,
    key_page_cache,
    value_page_cache,
    request_pages,
    context_length,
    output_weight,
    adapter_down_weight,
    adapter_up_weight,
    residual,
    host_slot_adapter,
    request_slot,
):
    n_hst, n_tp = lax.axis_size("hst"), lax.axis_size("tp")
    rows, width = queries.shape
    any_spec = pl.BlockSpec(memory_space=pl.ANY)
    dma = pltpu.SemaphoreType.DMA
    block = (n_hst, 16, width // 2)
    part_rows = n_hst * 8 // GROUPS // 2
    arguments = (
        queries,
        key_page_cache,
        value_page_cache,
        request_pages.T,
        context_length.reshape(1, -1),
        output_weight,
        adapter_down_weight,
        adapter_up_weight,
        host_slot_adapter.reshape(1, -1),
        request_slot.T,
    )
    summed = pl.pallas_call(
        functools.partial(kernel, n_hst, n_tp),
        out_shape=jax.ShapeDtypeStruct((rows, width), F32),
        in_specs=[any_spec] * len(arguments),
        out_specs=pl.BlockSpec(memory_space=pltpu.VMEM),
        scratch_shapes=[
            pltpu.SMEM(request_pages.shape[::-1], jnp.int32),
            pltpu.VMEM((1, rows), jnp.int32),
            pltpu.VMEM((1, host_slot_adapter.shape[0]), jnp.int32),
            pltpu.VMEM((1, rows), jnp.int32),
            pltpu.VMEM(queries.shape, BF),
            pltpu.VMEM((rows * width // HD, HD), F32),
            pltpu.VMEM(key_page_cache.shape, BF),
            pltpu.VMEM(value_page_cache.shape, BF),
            pltpu.VMEM(output_weight.shape, BF),
            pltpu.VMEM(adapter_down_weight.shape, BF),
            pltpu.VMEM(adapter_up_weight.shape, BF),
            pltpu.VMEM(queries.shape, F32),
            pltpu.VMEM((8, 128), jnp.int32),
            pltpu.VMEM((n_hst, 128), jnp.int32),
            pltpu.VMEM(block, BF),
            pltpu.VMEM(block, BF),
            pltpu.VMEM(block, BF),
            pltpu.VMEM(block, BF),
            pltpu.VMEM((n_tp // 2, rows, width), BF),
            pltpu.VMEM((n_tp // 2, rows, width), BF),
            pltpu.VMEM((n_tp // 2, rows, width), F32),
            pltpu.VMEM((n_tp // 2 - 1, rows, width), BF),
            pltpu.VMEM((n_tp // 2 - 1, rows, width), BF),
            pltpu.VMEM((GROUPS, part_rows, 128), BF),
            pltpu.VMEM((GROUPS, n_tp - 1, part_rows, 128), BF),
            dma((10,)),
            dma,
            dma((GROUPS,)),
            dma,
            dma((GROUPS,)),
            dma,
            dma((GROUPS,)),
            dma,
            dma,
            dma,
            dma,
            dma,
            dma((GROUPS,)),
        ],
        compiler_params=pltpu.CompilerParams(
            collective_id=0, has_side_effects=True, vmem_limit_bytes=40 * 1024 * 1024
        ),
        cost_estimate=pl.CostEstimate(
            flops=2_000_000_000, bytes_accessed=12_000_000, transcendentals=32768
        ),
        name="decode_step",
    )(*(pltpu.with_memory_space_constraint(a, pltpu.HBM) for a in arguments))
    return (residual.astype(F32) + summed).astype(BF)


def solution(mesh):
    in_specs = (
        P("hst", "tp"),
        P("hst", None, "tp"),
        P("hst", None, "tp"),
        P("hst", None),
        P("hst"),
        P("tp", None),
        P("hst", None, "tp"),
        P("hst", None, "tp"),
        P("hst", "tp"),
        P("hst"),
        P("hst", None),
    )
    out_specs = P("hst", "tp")
    return jax.shard_map(local, mesh=mesh, in_specs=in_specs, out_specs=out_specs, check_vma=False)
```

```python
import functools
import math

import jax
import jax.numpy as jnp
from jax import lax
from jax.experimental import pallas as pl
from jax.experimental.pallas import tpu as pltpu
from jax.sharding import PartitionSpec as P

HD = 128
ADAPTER_SCALE = 2.0
Z, X = 8, 4
GROUPS = 4
MESH = pl.DeviceIdType.MESH
BF = jnp.bfloat16
F32 = jnp.float32
NT = (((1,), (1,)), ((), ()))
NN = (((1,), (0,)), ((), ()))


def dot(a, b, dims=NN):
    return lax.dot_general(a, b, dims, preferred_element_type=F32)


def iota(shape, dim):
    return lax.broadcasted_iota(jnp.int32, shape, dim)


def offsets(step):
    i, j = step // Z, step % Z
    dz = Z // 2 + (1 - 2 * (j % 2)) * ((j + 1) // 2)
    return dz, (2, 3, 1, 0)[i]


def ahead_of(host, step):
    dz, dx = offsets(step)
    return lax.rem(host // X + dz, Z) * X + lax.rem(lax.rem(host, X) + dx, X)


def behind(host, step):
    dz, dx = offsets(step)
    return lax.rem(host // X + Z - dz, Z) * X + lax.rem(lax.rem(host, X) + X - dx, X)


def kernel(
    n_hst,
    n_tp,
    q_hbm,
    k_hbm,
    v_hbm,
    pages_hbm,
    length_hbm,
    w_hbm,
    down_hbm,
    up_hbm,
    table_hbm,
    slot_hbm,
    out_ref,
    pages_ref,
    length_ref,
    table_ref,
    slot_ref,
    q_ref,
    logits_ref,
    k_ref,
    v_ref,
    w_ref,
    down_ref,
    up_ref,
    att_ref,
    table_out,
    tables,
    rows_out,
    rows_in,
    back_out,
    back_in,
    pair_out,
    pair_in,
    base_own,
    base_out,
    base_in,
    part_out,
    part_in,
    local_sem,
    table_send,
    table_recv,
    rows_send,
    rows_recv,
    back_send,
    back_recv,
    pair_send,
    pair_recv,
    base_send,
    base_recv,
    part_send,
    part_recv,
):
    host = lax.axis_index("hst")
    lane = lax.axis_index("tp")

    def load(src, dst, i):
        return pltpu.make_async_copy(src, dst, local_sem.at[i])

    load_table = load(table_hbm, table_ref, 0)
    load_slot = load(slot_hbm, slot_ref, 1)
    load_pages = load(pages_hbm, pages_ref, 2)
    load_length = load(length_hbm, length_ref, 3)
    load_q = load(q_hbm, q_ref, 4)
    load_k = load(k_hbm, k_ref, 5)
    load_v = load(v_hbm, v_ref, 6)
    load_w = load(w_hbm, w_ref, 7)
    load_down = load(down_hbm, down_ref, 8)
    load_up = load(up_hbm, up_ref, 9)
    load_pages.start()
    load_q.start()
    load_k.start()
    load_length.start()
    load_table.start()
    load_slot.start()
    load_v.start()

    barrier = pltpu.get_barrier_semaphore()

    def greet_hosts(step):
        other = ahead_of(host, step)
        pl.semaphore_signal(barrier, inc=1, device_id=(other, lane), device_id_type=MESH)

    def greet_lanes(step):
        other = lax.rem(lane + step, n_tp)
        pl.semaphore_signal(barrier, inc=1, device_id=(host, other), device_id_type=MESH)

    for step in range(n_hst - 1):
        greet_hosts(step)
    for step in range(1, n_tp):
        greet_lanes(step)

    slots = table_ref.shape[1]
    row_total = slot_ref.shape[1]
    load_table.wait()
    load_slot.wait()
    table_out[...] = jnp.full(table_out.shape, -1, jnp.int32)
    table_out[0:1, 0:slots] = table_ref[...]
    table_row = table_out[0:1, :]
    owner_row = jnp.right_shift(table_row, 5)
    owner_all = jnp.broadcast_to(owner_row, (128, 128))
    s_sub, s_lane = iota((128, 128), 0), iota((128, 128), 1)
    owner_col = jnp.sum(jnp.where(s_sub == s_lane, owner_all, 0), axis=1, keepdims=True)
    place_row = jnp.sum(
        jnp.where((owner_col == owner_all) & (s_sub < s_lane), 1, 0), axis=0, keepdims=True
    )
    dz = jnp.bitwise_and(jnp.right_shift(owner_row, 2) - host // X + Z, Z - 1)
    dx = jnp.bitwise_and(jnp.bitwise_and(owner_row, X - 1) - lax.rem(host, X) + X, X - 1)
    z_order = jnp.where(dz >= Z // 2, 2 * dz - Z, Z - 1 - 2 * dz)
    x_order = jnp.where(dx >= X // 2, dx - X // 2, X - 1 - dx)
    start_row = (x_order * Z + z_order) * 8 + place_row * 4
    chosen_row = slot_ref[...]
    r_sub, r_lane = iota((row_total, 128), 0), iota((row_total, 128), 1)
    q_sub, q_lane = iota((row_total, row_total), 0), iota((row_total, row_total), 1)
    chosen_col = jnp.sum(jnp.where(q_sub == q_lane, chosen_row, 0), axis=1, keepdims=True)
    before_col = jnp.sum(
        jnp.where((chosen_col == chosen_row) & (q_lane < q_sub), 1, 0), axis=1, keepdims=True
    )
    target_col = before_col + jnp.sum(
        jnp.where(chosen_col == r_lane, start_row, 0), axis=1, keepdims=True
    )
    target_row = jnp.sum(jnp.where(r_sub == r_lane, target_col, 0), axis=0, keepdims=True)
    send_total = n_hst * 8
    scatter = jnp.where(
        iota((send_total, row_total), 0) == target_row[:, :row_total], 1.0, 0.0
    ).astype(BF)
    back_place = (target_col // 8) * 16 + lax.rem(target_col, 8)
    back_lane = iota((row_total, n_hst * 16), 1)
    gather_lo = jnp.where(back_lane == back_place, 1.0, 0.0).astype(BF)
    gather_hi = jnp.where(back_lane == back_place + 8, 1.0, 0.0).astype(BF)

    heads = q_ref.shape[1] // HD
    tall = heads * 8
    load_length.wait()
    row = iota((row_total * heads, row_total), 0)
    request = row // tall * 8 + lax.rem(row, 8)
    length_col = jnp.sum(
        jnp.where(iota(row.shape, 1) == request, length_ref[...], 0), axis=1, keepdims=True
    )

    load_pages.wait()
    load_q.wait()
    load_k.wait()
    load_w.start()
    load_down.start()
    load_up.start()
    sub = iota((8, HD), 0)

    def pages_of(ref, row):
        return [ref[pages_ref[p, row]] for p in range(pages_ref.shape[0])]

    def pair_of(ref, row):
        return jnp.concatenate(pages_of(ref, row) + pages_of(ref, row + 1), axis=0)

    def match(step, carry):
        first = pl.multiple_of(step * 16, 16)
        q16 = q_ref[pl.ds(first, 16), :].astype(F32)
        for part in range(2):
            q = q16[part * 8 : (part + 1) * 8]
            q = jnp.concatenate([q[:, j * HD : (j + 1) * HD] for j in range(heads)], axis=0).astype(BF)
            got = [jnp.zeros((8, HD), F32)] * heads
            for r in range(0, 8, 2):
                s = dot(q, pair_of(k_ref, first + part * 8 + r), NT)
                for j in range(heads):
                    rows8 = s[j * 8 : (j + 1) * 8]
                    got[j] = jnp.where(sub == r, rows8[:, :HD], got[j])
                    got[j] = jnp.where(sub == r + 1, rows8[:, HD:], got[j])
            logits_ref[pl.ds(pl.multiple_of((step * 2 + part) * tall, tall), tall), :] = jnp.concatenate(
                got, axis=0
            )
        return carry

    lax.fori_loop(0, row_total // 16, match, 0)

    live = iota((row_total * heads, HD), 1) < length_col
    logits = jnp.where(live, logits_ref[...] * (1.0 / math.sqrt(HD)), -jnp.inf)
    e = jnp.exp(logits - jnp.max(logits, axis=1, keepdims=True))
    logits_ref[...] = e / jnp.sum(e, axis=1, keepdims=True)

    load_v.wait()

    def blend(step, carry):
        first = pl.multiple_of(step * 16, 16)
        for part in range(2):
            p = logits_ref[pl.ds(pl.multiple_of((step * 2 + part) * tall, tall), tall), :]
            p = [p[j * 8 : (j + 1) * 8] for j in range(heads)]
            acc = jnp.zeros((tall, HD), F32)
            for r in range(0, 8, 2):
                spread = jnp.concatenate(
                    [
                        jnp.concatenate([jnp.where(sub == r + i, x, 0.0) for x in p], axis=0)
                        for i in range(2)
                    ],
                    axis=1,
                )
                acc = acc + dot(spread.astype(BF), pair_of(v_ref, first + part * 8 + r))
            for j in range(heads):
                att_ref[pl.ds(first + part * 8, 8), j * HD : (j + 1) * HD] = acc[j * 8 : (j + 1) * 8]
        return carry

    lax.fori_loop(0, row_total // 16, blend, 0)

    att = att_ref[...].astype(BF)
    half = att.shape[1] // 2

    def pack(lo, hi):
        blocks = lo.shape[0] // 8
        return jnp.concatenate(
            [lo.reshape(blocks, 8, half), hi.reshape(blocks, 8, half)], axis=1
        ).astype(BF)

    def unpack(x):
        rows = x.shape[0] * 8
        x = x.astype(F32)
        lo, hi = x[:, :8].reshape(rows, half), x[:, 8:].reshape(rows, half)
        return jnp.concatenate([lo, hi], axis=1).astype(BF)


    def arrived(ref, sem):
        pltpu.make_async_copy(ref, ref, sem).wait()

    def table_copy(step, group):
        return pltpu.make_async_remote_copy(
            src_ref=table_out.at[0:1, :],
            dst_ref=tables.at[pl.ds(step, 1), :],
            send_sem=table_send,
            recv_sem=table_recv.at[group],
            device_id=(ahead_of(host, step), lane),
            device_id_type=MESH,
        )

    def rows_copy(step, group):
        return pltpu.make_async_remote_copy(
            src_ref=rows_out.at[step],
            dst_ref=rows_in.at[step],
            send_sem=rows_send,
            recv_sem=rows_recv.at[group],
            device_id=(ahead_of(host, step), lane),
            device_id_type=MESH,
        )

    group_hosts = n_hst // GROUPS
    last = n_hst - 1

    pl.semaphore_wait(barrier, n_hst - 1 + n_tp - 1)
    for group in range(GROUPS):
        first = group * group_hosts
        spread = dot(scatter[first * 8 : (first + group_hosts) * 8], att)
        rows_out[first : first + group_hosts] = pack(spread[:, :half], spread[:, half:])
        for step in range(first, min(first + group_hosts, last)):
            table_copy(step, group).start()
            rows_copy(step, group).start()
    pltpu.make_async_copy(
        table_out.at[0:1, :], tables.at[last : last + 1, :], table_recv.at[GROUPS - 1]
    ).start()
    pltpu.make_async_copy(rows_out.at[last], rows_in.at[last], rows_recv.at[GROUPS - 1]).start()

    load_w.wait()
    width = out_ref.shape[1]
    chips = n_tp // 2
    chip, core = lane // 2, lax.rem(lane, 2)
    turns = (2, 1, 3, 0)

    def project(which):
        return dot(att, w_ref[:, pl.ds(pl.multiple_of(which * width, width), width)])

    def chip_at(turn):
        return lax.rem(chip + turn, chips)

    def pair_copy():
        return pltpu.make_async_remote_copy(
            src_ref=pair_out,
            dst_ref=pair_in,
            send_sem=pair_send,
            recv_sem=pair_recv,
            device_id=(host, lane + 1 - 2 * core),
            device_id_type=MESH,
        )

    def base_copy(i):
        return pltpu.make_async_remote_copy(
            src_ref=base_out.at[i],
            dst_ref=base_in.at[i],
            send_sem=base_send,
            recv_sem=base_recv,
            device_id=(host, 2 * chip_at(turns[i]) + core),
            device_id_type=MESH,
        )

    for i, turn in enumerate(turns):
        pair_out[i] = project(2 * chip_at(turn) + 1 - core).astype(BF)
    pair_copy().start()
    for i, turn in enumerate(turns):
        base_own[i] = project(2 * chip_at(turn) + core)
    pair_copy().wait()
    for i in range(chips - 1):
        base_out[i] = (base_own[i] + pair_in[i].astype(F32)).astype(BF)
        base_copy(i).start()
    out_ref[...] = base_own[chips - 1] + pair_in[chips - 1].astype(F32)

    group_rows = group_hosts * 8
    owned_total, rank, _ = down_ref.shape
    place_sub, place_lane = iota((group_rows, 128), 0), iota((group_rows, 128), 1)
    from_host = iota((group_rows, group_hosts), 0) // 8 == iota((group_rows, group_hosts), 1)
    from_host = jnp.where(from_host, 1.0, 0.0).astype(BF)
    earlier = jnp.where(s_sub < s_lane, 1.0, 0.0).astype(BF)

    def adapters(group):
        first = group * group_hosts
        table = tables[first : first + group_hosts]
        owned = jnp.right_shift(table, 5) == host
        ahead = dot(jnp.where(owned, 1.0, 0.0).astype(BF), earlier)
        local_index = jnp.bitwise_and(table, 31).astype(F32)

        def place_index(place):
            got = jnp.where(owned & (ahead == place), local_index, -1.0)
            got = jnp.broadcast_to(jnp.max(got, axis=1, keepdims=True), got.shape).astype(BF)
            return dot(from_host, got)

        found = jnp.where(lax.rem(place_sub, 8) < 4, place_index(0.0), place_index(1.0))
        return found - jnp.where(place_lane >= 64, 1.0, 0.0), found.T[:rank]


    def part_copy(group, step):
        return pltpu.make_async_remote_copy(
            src_ref=part_out.at[group],
            dst_ref=part_in.at[group, step - 1],
            send_sem=part_send,
            recv_sem=part_recv.at[group],
            device_id=(host, lax.rem(lane + step, n_tp)),
            device_id_type=MESH,
        )

    load_down.wait()
    own_part, adapter = {}, {}
    for group in range(GROUPS):
        first = group * group_hosts
        arrived(tables.at[first : first + group_hosts], table_recv.at[group])
        adapter[group], adapter_lane = adapters(group)
        arrived(rows_in.at[first : first + group_hosts], rows_recv.at[group])
        x = unpack(rows_in[first : first + group_hosts])
        folded = jnp.zeros((rank, group_rows), F32)
        for c in range(0, owned_total, 2):
            s = dot(down_ref[c : c + 2].reshape(2 * rank, 2 * half), x, NT)
            for i in range(2):
                folded = folded + jnp.where(
                    adapter_lane == float(c + i), s[i * rank : (i + 1) * rank], 0.0
                )
        own_part[group] = folded
        part_out[group] = jnp.concatenate([folded[: rank // 2], folded[rank // 2 :]], axis=1).astype(BF)
        for step in (4, 5, 3, 2, 6, 7, 1):
            part_copy(group, step).start()

    arrived(base_in, base_recv)
    base = out_ref[...]
    for i in range(chips - 1):
        base = base + base_in[i].astype(F32)
    out_ref[...] = base

    def back_copy(step, group):
        other = behind(host, step)
        return pltpu.make_async_remote_copy(
            src_ref=back_out.at[step],
            dst_ref=back_in.at[step],
            send_sem=back_send,
            recv_sem=back_recv.at[group],
            device_id=(other, lane),
            device_id_type=MESH,
        )

    load_up.wait()
    for group in range(GROUPS):
        arrived(part_in.at[group], part_recv.at[group])
        g = part_in[group, 0].astype(F32)
        for step in range(2, n_tp):
            g = g + part_in[group, step - 1].astype(F32)
        g = own_part[group] + jnp.concatenate([g[:, :group_rows], g[:, group_rows:]], axis=0)
        full = jnp.concatenate([g, g], axis=0).T
        spread_up = jnp.concatenate(
            [jnp.where(adapter[group] == float(c), full, 0.0) for c in range(0, owned_total, 2)], axis=1
        )
        raised = dot(spread_up.astype(BF), up_ref[...].reshape(owned_total * rank, 2 * half))
        first = group * group_hosts
        back_out[first : first + group_hosts] = pack(raised[:, :half], raised[:, half:])
        for step in range(first, min(first + group_hosts, last)):
            back_copy(step, group).start()

    pltpu.make_async_copy(back_out.at[last], back_in.at[last], back_recv.at[GROUPS - 1]).start()
    given_lo, given_hi = 0.0, 0.0
    for group in range(GROUPS):
        first = group * group_hosts
        arrived(back_in.at[first : first + group_hosts], back_recv.at[group])
        y = back_in[first : first + group_hosts].reshape(group_hosts * 16, half)
        mine = slice(first * 16, (first + group_hosts) * 16)
        given_lo = given_lo + dot(gather_lo[:, mine], y)
        given_hi = given_hi + dot(gather_hi[:, mine], y)
    out_ref[:, :half] += ADAPTER_SCALE * given_lo
    out_ref[:, half:] += ADAPTER_SCALE * given_hi

    arrived(tables.at[0:last], table_send)
    arrived(rows_out.at[0:last], rows_send)
    arrived(back_out.at[0:last], back_send)
    arrived(base_out, base_send)
    arrived(part_in, part_send)


def local(
    queries,
    key_page_cache,
    value_page_cache,
    request_pages,
    context_length,
    output_weight,
    adapter_down_weight,
    adapter_up_weight,
    residual,
    host_slot_adapter,
    request_slot,
):
    n_hst, n_tp = lax.axis_size("hst"), lax.axis_size("tp")
    rows, width = queries.shape
    any_spec = pl.BlockSpec(memory_space=pl.ANY)
    dma = pltpu.SemaphoreType.DMA
    block = (n_hst, 16, width // 2)
    part_rows = n_hst * 8 // GROUPS // 2
    arguments = (
        queries,
        key_page_cache,
        value_page_cache,
        request_pages.T,
        context_length.reshape(1, -1),
        output_weight,
        adapter_down_weight,
        adapter_up_weight,
        host_slot_adapter.reshape(1, -1),
        request_slot.T,
    )
    summed = pl.pallas_call(
        functools.partial(kernel, n_hst, n_tp),
        out_shape=jax.ShapeDtypeStruct((rows, width), F32),
        in_specs=[any_spec] * len(arguments),
        out_specs=pl.BlockSpec(memory_space=pltpu.VMEM),
        scratch_shapes=[
            pltpu.SMEM(request_pages.shape[::-1], jnp.int32),
            pltpu.VMEM((1, rows), jnp.int32),
            pltpu.VMEM((1, host_slot_adapter.shape[0]), jnp.int32),
            pltpu.VMEM((1, rows), jnp.int32),
            pltpu.VMEM(queries.shape, BF),
            pltpu.VMEM((rows * width // HD, HD), F32),
            pltpu.VMEM(key_page_cache.shape, BF),
            pltpu.VMEM(value_page_cache.shape, BF),
            pltpu.VMEM(output_weight.shape, BF),
            pltpu.VMEM(adapter_down_weight.shape, BF),
            pltpu.VMEM(adapter_up_weight.shape, BF),
            pltpu.VMEM(queries.shape, F32),
            pltpu.VMEM((8, 128), jnp.int32),
            pltpu.VMEM((n_hst, 128), jnp.int32),
            pltpu.VMEM(block, BF),
            pltpu.VMEM(block, BF),
            pltpu.VMEM(block, BF),
            pltpu.VMEM(block, BF),
            pltpu.VMEM((n_tp // 2, rows, width), BF),
            pltpu.VMEM((n_tp // 2, rows, width), BF),
            pltpu.VMEM((n_tp // 2, rows, width), F32),
            pltpu.VMEM((n_tp // 2 - 1, rows, width), BF),
            pltpu.VMEM((n_tp // 2 - 1, rows, width), BF),
            pltpu.VMEM((GROUPS, part_rows, 128), BF),
            pltpu.VMEM((GROUPS, n_tp - 1, part_rows, 128), BF),
            dma((10,)),
            dma,
            dma((GROUPS,)),
            dma,
            dma((GROUPS,)),
            dma,
            dma((GROUPS,)),
            dma,
            dma,
            dma,
            dma,
            dma,
            dma((GROUPS,)),
        ],
        compiler_params=pltpu.CompilerParams(
            collective_id=0, has_side_effects=True, vmem_limit_bytes=40 * 1024 * 1024
        ),
        cost_estimate=pl.CostEstimate(
            flops=2_000_000_000, bytes_accessed=12_000_000, transcendentals=32768
        ),
        name="decode_step",
    )(*(pltpu.with_memory_space_constraint(a, pltpu.HBM) for a in arguments))
    return (residual.astype(F32) + summed).astype(BF)


def solution(mesh):
    in_specs = (
        P("hst", "tp"),
        P("hst", None, "tp"),
        P("hst", None, "tp"),
        P("hst", None),
        P("hst"),
        P("tp", None),
        P("hst", None, "tp"),
        P("hst", None, "tp"),
        P("hst", "tp"),
        P("hst"),
        P("hst", None),
    )
    out_specs = P("hst", "tp")
    return jax.shard_map(local, mesh=mesh, in_specs=in_specs, out_specs=out_specs, check_vma=False)
```
